512 devices in a mesh: wide: 32 (over y, z_hi, core), narrow: 16 (over z_lo, x).
Axes of the slice: x: 4, y: 8, z: 8 (z_hi: 2, z_lo: 4; z = z_hi * 4 + z_lo), core: 2. Of those that a mesh axis runs over, the one named last changes fastest.
Arguments:
- pooled: bfloat16 [262144, 1024], P(('wide', 'narrow')), may hold values from -6 to 6
- cotangent: bfloat16 [262144, 512], P(('wide', 'narrow')), may hold values from -6 to 6
- w_first: bfloat16 [1024, 1024], P('narrow'), may hold values from -0.1875 to 0.1875
- b_first: float32 [1024], replicated, may hold values from -5 to 5
- w_second: bfloat16 [1024, 512], P('narrow'), may hold values from -0.1875 to 0.1875
- counts: bfloat16 [8, 256, 262144], P(None, 'narrow', 'wide'), may hold values from 0 to 3, as said below
- row_ids: int32 [8, 256], P(None, 'narrow'), may hold values from 0 to 63, as said below
- table: float32 [8, 1024, 128], P(None, 'narrow'), may hold values from -6 to 6
- accum: float32 [8, 1024, 128], P(None, 'narrow'), may hold values from 0.1 to 10
Outputs:
- new_table: float32 [8, 1024, 128], P(None, 'narrow')
- new_accum: float32 [8, 1024, 128], P(None, 'narrow')
The draws below stay inside these ranges and needn't reach their ends.
Inputs may be any that keep to these rules, and one draw needn't show every extreme that they name: `counts`: each entry is zero where the sample does not look up the active row, else a positive lookup weight. `row_ids`: for each table, the 16 ids of one owner (slots j * 16 to (j + 1) * 16 - 1) are distinct.
All inputs are finite; a program needn't handle non-finite values.
Results may differ from the reference program's by a relative error of at most 0.0038.
Values may be sent and summed in bfloat16 or wider, within the bound.
No kernel may reach another device: no remote copies, remote signals or barrier semaphores. Data moves between devices by JAX's collectives and lax.ppermute only.
A program may use at most 128 MiB of HBM per device.

```python
import math
import jax
import jax.numpy as jnp
from jax import lax

TABLES = 8
EMB = 128
INNER = 1024
TOP = 512
ACT = 16
ROWS_DEV = 64
EMB_ALL = 1024
GROUP_BAGS = 8192
SAMPLES = 262144
N_WIDE = 32
N_NARROW = 16


def draw_counts(key, part):
    level_key = jax.random.fold_in(key, 11)
    hit_key = jax.random.fold_in(key, 12)
    value_key = jax.random.fold_in(key, 13)
    shape = (TABLES, N_NARROW * ACT, N_WIDE * GROUP_BAGS)
    levels = jax.random.randint(level_key, (TABLES, N_NARROW * ACT, 1), 0, 4)
    limits = jnp.right_shift(jnp.int32(1024), levels.astype(jnp.int32))
    hits = jax.random.randint(hit_key, shape, 0, 1024) < limits
    values = 0.25 + 2.75 * jax.random.uniform(value_key, shape, jnp.float32)
    return jnp.where(hits, values, jnp.float32(0.0)).astype(jnp.bfloat16)


def pick_rows(subkey):
    return jax.random.permutation(subkey, ROWS_DEV)[:ACT]


def draw_row_ids(key, part):
    keys = jax.random.split(jax.random.fold_in(key, 21), TABLES * N_NARROW)
    picks = jax.vmap(pick_rows)(keys)
    return picks.reshape(TABLES, N_NARROW * ACT).astype(jnp.int32)


def shard_levels(key, shape, pieces, least, high):
    level = 1.0
    for axis_at, blocks in pieces:
        steps = jax.random.uniform(jax.random.fold_in(jax.random.fold_in(key, 6), axis_at), (blocks,), jnp.float32, least / len(pieces), high / len(pieces))
        level = level * jnp.repeat(jnp.exp(steps), shape[axis_at] // blocks).reshape((-1,) + (1,) * (len(shape) - 1 - axis_at))
    return level


def normal_values(rng, extent, scale, bound, shards=(), kind=jnp.bfloat16):
    gain = shard_levels(rng, extent, shards, -0.22, 0.18) if shards else 1.0
    array = jax.random.normal(rng, extent, jnp.float32) * scale * gain
    return jnp.minimum(jnp.maximum(array, -bound), bound).astype(kind)


def setup_inputs(seed: int = 0) -> dict:
    streams_of = jax.random.split(jax.random.key(seed), 10)
    pooled = normal_values(streams_of[0], (SAMPLES, EMB_ALL), 1.0, 6.0, ((0, 512),))
    cotangent = normal_values(streams_of[1], (SAMPLES, TOP), 1.0, 6.0, ((0, 512),))
    w_first = normal_values(streams_of[2], (EMB_ALL, INNER), EMB_ALL ** -0.5, 0.1875, ((0, 16),))
    b_first = normal_values(streams_of[3], (INNER,), 1.0, 5.0, (), jnp.float32)
    w_second = normal_values(streams_of[4], (INNER, TOP), INNER ** -0.5, 0.1875, ((0, 16),))
    counts = draw_counts(jax.random.fold_in(streams_of[9], 71), 0)
    row_ids = draw_row_ids(jax.random.fold_in(streams_of[9], 71), 0)
    table = normal_values(streams_of[7], (TABLES, N_NARROW * ROWS_DEV, EMB), 1.0, 6.0, ((1, 16),), jnp.float32)
    accum = jnp.clip(jnp.exp(math.log(10.0) - 4.6051702 * jax.random.uniform(streams_of[8], (TABLES, N_NARROW * ROWS_DEV, EMB), jnp.float32) ** shard_levels(streams_of[8], (TABLES, N_NARROW * ROWS_DEV, EMB), ((1, 16),), -0.2, 0.2)), 0.1, 10.0)
    return dict(pooled=pooled, cotangent=cotangent, w_first=w_first, b_first=b_first, w_second=w_second, counts=counts, row_ids=row_ids, table=table, accum=accum)


clip_factor = 0.5
learn_rate = 0.05
epsilon = 1e-08

def tower_back(inputs, cotangent, w_first, b_first, w_second):
    hidden_in = jnp.dot(inputs, w_first, preferred_element_type=jnp.float32) + b_first
    back_hidden = lax.dot_general(cotangent, w_second, (((1,), (1,)), ((), ())), preferred_element_type=jnp.float32)
    sigmoid_val = jax.nn.sigmoid(hidden_in)
    slopes = sigmoid_val * (1.0 + hidden_in * (1.0 - sigmoid_val))
    deltas = (back_hidden * slopes).astype(jnp.bfloat16)
    return lax.dot_general(deltas, w_first, (((1,), (1,)), ((), ())), preferred_element_type=jnp.float32).astype(jnp.bfloat16)

def clip_rows(grads, limit):
    norms = jnp.sqrt(lax.optimization_barrier(jnp.sum(grads * grads, axis=-1, keepdims=True)))
    return grads * (limit / jnp.maximum(norms, limit))

def reference(pooled, cotangent, w_first, b_first, w_second, counts, row_ids, table, accum):
    tables = counts.shape[0]
    emb = table.shape[2]
    bags = counts.shape[2] // N_WIDE
    scale = 1.0 / math.sqrt(bags)
    limit = clip_factor * math.sqrt(emb)

    def one_group(group_index):
        offset = group_index * bags
        inputs = lax.dynamic_slice_in_dim(pooled, offset, bags, 0)
        upstream = lax.dynamic_slice_in_dim(cotangent, offset, bags, 0)
        grad_in = tower_back(inputs, upstream, w_first, b_first, w_second)
        lookups = lax.dynamic_slice_in_dim(counts, offset, bags, 2)
        grads = jnp.stack([jnp.dot(lookups[table_no], grad_in[:, table_no * emb:(table_no + 1) * emb], preferred_element_type=jnp.float32) for table_no in range(tables)])
        return clip_rows(grads * scale, limit)
    summed = lax.optimization_barrier(jnp.sum(lax.map(one_group, jnp.arange(N_WIDE, dtype=jnp.int32)), axis=0))
    slots = row_ids.shape[1]
    owners = jnp.arange(slots, dtype=jnp.int32) // ACT
    rows_global = (owners * ROWS_DEV)[None, :] + row_ids
    table_index = jnp.arange(tables, dtype=jnp.int32)[:, None]
    current = table[table_index, rows_global]
    old_acc = accum[table_index, rows_global]
    new_acc = old_acc + summed * summed
    new_rows = current - learn_rate * summed / (jnp.sqrt(new_acc) + epsilon)
    new_table = table.at[table_index, rows_global].set(new_rows)
    new_accum = accum.at[table_index, rows_global].set(new_acc)
    return (new_table, new_accum)
```

```python
import functools
import math

import jax
import jax.numpy as jnp
from jax import lax
from jax.experimental import pallas as pl
from jax.experimental.pallas import tpu as pltpu
from jax.sharding import PartitionSpec as P

clip_factor = 0.5
learn_rate = 0.05
epsilon = 1e-08

N_Y, N_HI, N_CORE = 8, 2, 2
bf16, f32 = jnp.bfloat16, jnp.float32
VMEM = pl.BlockSpec(memory_space=pltpu.VMEM)
SMEM = pl.BlockSpec(memory_space=pltpu.SMEM)
MIB = 1 << 20


def wide_at(y, hi, core):
    return (y * N_HI + hi) * N_CORE + core


Y_GROUPS = [[wide_at(y, h, c) for y in range(N_Y)] for h in range(N_HI) for c in range(N_CORE)]
YZ_GROUPS = [[wide_at(y, h, c) for y in range(N_Y) for h in range(N_HI)] for c in range(N_CORE)]
CORE_SWAP = [(w, w ^ 1) for w in range(N_Y * N_HI * N_CORE)]


def call(body, out_shape, in_specs, scratch=(), flops=0, nbytes=0, limit=48):
    return pl.pallas_call(
        body,
        out_shape=out_shape,
        in_specs=in_specs,
        out_specs=jax.tree.map(lambda _: VMEM, out_shape),
        scratch_shapes=list(scratch),
        compiler_params=pltpu.CompilerParams(vmem_limit_bytes=limit * MIB),
        cost_estimate=pl.CostEstimate(flops=flops, bytes_accessed=nbytes, transcendentals=0),
    )


def tower_body(core_ref, own_ref, other_ref, pooled_ref, cot_ref, bias_ref, grad_ref, first, second, deltas):
    core = core_ref[0]
    owners = own_ref.shape[1]
    rows = first.shape[0] // owners
    half = rows // 2
    for ref, side in ((own_ref, core), (other_ref, 1 - core)):
        for n in range(owners):
            at = pl.multiple_of(n * rows + side * half, 32)
            for y in range(N_Y):
                first[pl.ds(at, half), y * 128 : (y + 1) * 128] = ref[y, n, :half, :]
                lower = pl.multiple_of(at + (y % 2) * 16, 16)
                second[pl.ds(lower, 16), (y // 2) * 128 : (y // 2 + 1) * 128] = ref[y, n, half:, :]
    inner = first.shape[1]
    step = 256
    across = (((1,), (1,)), ((), ()))
    for at in range(0, inner, step):
        cols = slice(at, at + step)
        hidden = jnp.dot(pooled_ref[...], first[:, cols], preferred_element_type=f32) + bias_ref[:, cols]
        back = lax.dot_general(cot_ref[...], second[cols, :], across, preferred_element_type=f32)
        gate = jax.nn.sigmoid(hidden)
        deltas[:, cols] = (back * (gate * (1.0 + hidden * (1.0 - gate)))).astype(bf16)
    for at in range(0, first.shape[0], step):
        cols = slice(at, at + step)
        grad_ref[:, cols] = lax.dot_general(
            deltas[...], first[cols, :], across, preferred_element_type=f32
        ).astype(bf16)


def partial_body(counts_ref, grad_ref, out_ref):
    owners, tables, act, bags = counts_ref.shape
    emb = grad_ref.shape[1] // tables
    for t in range(tables):
        cols = slice(t * emb, (t + 1) * emb)
        lookups = counts_ref[:, t, :, :].reshape(owners * act, bags)
        part = jnp.dot(lookups, grad_ref[:, cols], preferred_element_type=f32)
        out_ref[:, :, cols] = part.reshape(owners, act, emb).astype(bf16)


def clip_body(scale, limit, core_ref, parts_ref, keep_ref, send_ref, rows):
    peers, act, width = parts_ref.shape
    emb = rows.shape[1]
    total = parts_ref[0].astype(f32)
    for n in range(1, peers):
        total = total + parts_ref[n].astype(f32)
    total = total * scale
    for t in range(width // emb):
        grads = total[:, t * emb : (t + 1) * emb]
        norms = jnp.sqrt(jnp.sum(grads * grads, axis=-1, keepdims=True))
        rows[t * act : (t + 1) * act, :] = grads * (limit / jnp.maximum(norms, limit))
    core = core_ref[0]
    half = rows.shape[0] // 2
    keep_ref[...] = rows[pl.ds(pl.multiple_of(core * half, 8), half), :]
    send_ref[...] = rows[pl.ds(pl.multiple_of((1 - core) * half, 8), half), :]


def pair_body(keep_ref, got_ref, out_ref):
    both = (keep_ref[...] + got_ref[...]).astype(bf16)
    for n in range(out_ref.shape[0]):
        out_ref[n] = both


def share_body(parts_ref, out_ref):
    total = parts_ref[0].astype(f32)
    for n in range(1, parts_ref.shape[0]):
        total = total + parts_ref[n].astype(f32)
    out_ref[...] = total


def update_body(core_ref, ids_ref, mine_ref, other_ref, table_ref, accum_ref, new_table_ref, new_accum_ref, dense):
    tables, act = ids_ref.shape
    per_core = tables // 2
    core = core_ref[0]
    dense[...] = jnp.zeros_like(dense)
    for ref, side in ((mine_ref, core), (other_ref, 1 - core)):
        for t in range(per_core):
            for a in range(act):
                table = side * per_core + t
                row = ids_ref[table, a]
                dense[table, pl.ds(row, 1), :] = ref[pl.ds(t * act + a, 1), :]
    for t in range(tables):
        summed = dense[t]
        new_acc = accum_ref[t] + summed * summed
        new_accum_ref[t] = new_acc
        new_table_ref[t] = table_ref[t] - learn_rate * summed / (jnp.sqrt(new_acc) + epsilon)


def shards(pooled, cotangent, w_first, b_first, w_second, counts, row_ids, table, accum):
    tables, act, bags = counts.shape
    emb = table.shape[2]
    samples = pooled.shape[0]
    inner, top = w_first.shape[1], w_second.shape[1]
    owners = lax.axis_size("narrow")
    scale = 1.0 / math.sqrt(bags)
    limit = clip_factor * math.sqrt(emb)
    wide = lax.axis_index("wide")
    core = wide % N_CORE
    y = wide // (N_HI * N_CORE)
    core_at = core.reshape(1).astype(jnp.int32)

    half = w_first.shape[0] // 2
    piece = jnp.concatenate(
        [
            lax.dynamic_slice(w_first, (core * half, y * 128), (half, 128)),
            lax.dynamic_slice(w_second, (core * half + (y % 2) * 16, (y // 2) * 128), (16, 128)),
        ],
        axis=0,
    )
    spread = lax.all_to_all(
        jnp.broadcast_to(piece[None], (owners, *piece.shape)), "narrow", 0, 0, tiled=True
    )
    by_owner = jnp.transpose(counts.reshape(tables, act, owners, samples), (2, 0, 1, 3))
    by_owner, spread = lax.optimization_barrier((by_owner, spread))
    own = lax.all_gather(spread, "wide", axis=0, axis_index_groups=Y_GROUPS)
    regrouped = lax.all_to_all(by_owner, "narrow", 0, 0, tiled=True)
    other = lax.ppermute(own, "wide", CORE_SWAP)

    grad_in = call(
        tower_body,
        jax.ShapeDtypeStruct((samples, owners * w_first.shape[0]), bf16),
        [SMEM] + [VMEM] * 5,
        [
            pltpu.VMEM((owners * w_first.shape[0], inner), bf16),
            pltpu.VMEM((inner, top), bf16),
            pltpu.VMEM((samples, inner), bf16),
        ],
        flops=2 * samples * inner * (2 * inner + top),
        nbytes=8 * MIB,
    )(core_at, own, other, pooled, cotangent, b_first.reshape(1, -1))

    parts = call(
        partial_body,
        jax.ShapeDtypeStruct((owners, act, tables * emb), bf16),
        [VMEM] * 2,
        flops=2 * owners * act * samples * tables * emb,
        nbytes=4 * MIB,
    )(regrouped, grad_in)
    arrived = lax.all_to_all(parts, "narrow", 0, 0, tiled=True)

    rows = tables * act
    half_rows = jax.ShapeDtypeStruct((rows // 2, emb), f32)
    keep, send = call(
        functools.partial(clip_body, scale, limit),
        (half_rows, half_rows),
        [SMEM, VMEM],
        [pltpu.VMEM((rows, emb), f32)],
        nbytes=MIB,
    )(core_at, arrived)
    got = lax.ppermute(send, "wide", CORE_SWAP)
    copies = call(
        pair_body, jax.ShapeDtypeStruct((N_Y * N_HI, rows // 2, emb), bf16), [VMEM] * 2, nbytes=MIB
    )(keep, got)
    shares = lax.all_to_all(copies, "wide", 0, 0, axis_index_groups=YZ_GROUPS, tiled=True)
    mine = call(share_body, half_rows, [VMEM], nbytes=MIB)(shares)
    theirs = lax.ppermute(mine, "wide", CORE_SWAP)
    whole = jax.ShapeDtypeStruct(table.shape, f32)
    return call(
        update_body,
        (whole, whole),
        [SMEM, SMEM] + [VMEM] * 4,
        [pltpu.VMEM(table.shape, f32)],
        nbytes=2 * MIB,
    )(core_at, row_ids, mine, theirs, table, accum)


def solution(mesh):
    in_specs = (
        P(("wide", "narrow"), None),
        P(("wide", "narrow"), None),
        P("narrow", None),
        P(),
        P("narrow", None),
        P(None, "narrow", "wide"),
        P(None, "narrow"),
        P(None, "narrow", None),
        P(None, "narrow", None),
    )
    out_specs = (P(None, "narrow", None), P(None, "narrow", None))
    return jax.shard_map(shards, mesh=mesh, in_specs=in_specs, out_specs=out_specs, check_vma=False)
```

```python
import functools
import math

import jax
import jax.numpy as jnp
from jax import lax
from jax.experimental import pallas as pl
from jax.experimental.pallas import tpu as pltpu
from jax.sharding import PartitionSpec as P

clip_factor = 0.5
learn_rate = 0.05
epsilon = 1e-08

N_Y, N_HI, N_CORE = 8, 2, 2
bf16, f32 = jnp.bfloat16, jnp.float32
VMEM = pl.BlockSpec(memory_space=pltpu.VMEM)
SMEM = pl.BlockSpec(memory_space=pltpu.SMEM)
HBM = pl.BlockSpec(memory_space=pltpu.HBM)
MIB = 1 << 20


def wide_at(y, hi, core):
    return (y * N_HI + hi) * N_CORE + core


YC_GROUPS = [
    [wide_at(y, h, c) for y in range(N_Y) for c in range(N_CORE)] for h in range(N_HI)
]
YZ_GROUPS = [[wide_at(y, h, c) for y in range(N_Y) for h in range(N_HI)] for c in range(N_CORE)]
CORE_SWAP = [(w, w ^ 1) for w in range(N_Y * N_HI * N_CORE)]


def chip_pairs(owners):
    return [
        [wide_at(y, h, c) * owners + n for n in range(owners) for c in range(N_CORE)]
        for y in range(N_Y)
        for h in range(N_HI)
    ]


def call(body, out_shape, in_specs, scratch=(), flops=0, nbytes=0, limit=16):
    return pl.pallas_call(
        body,
        out_shape=out_shape,
        in_specs=in_specs,
        out_specs=jax.tree.map(lambda _: VMEM, out_shape),
        scratch_shapes=list(scratch),
        compiler_params=pltpu.CompilerParams(vmem_limit_bytes=limit * MIB),
        cost_estimate=pl.CostEstimate(flops=flops, bytes_accessed=nbytes, transcendentals=0),
    )


def piece_body(at_ref, first_ref, second_ref, out_ref, held, sems):
    core, y = at_ref[0], at_ref[1]
    half = first_ref.shape[0] // N_CORE
    top = pl.multiple_of(core * half, 32)
    low = pl.multiple_of(core * half + (y % 2) * 16, 16)
    copies = [
        pltpu.make_async_copy(
            first_ref.at[pl.ds(top, half), pl.ds(pl.multiple_of(y * 128, 128), 128)],
            held.at[pl.ds(0, half), :],
            sems.at[0],
        ),
        pltpu.make_async_copy(
            second_ref.at[pl.ds(low, 16), pl.ds(pl.multiple_of((y // 2) * 128, 128), 128)],
            held.at[pl.ds(half, 16), :],
            sems.at[1],
        ),
    ]
    for copy in copies:
        copy.start()
    for copy in copies:
        copy.wait()
    for n in range(out_ref.shape[0]):
        out_ref[n] = held[...]


def tower_body(pieces_ref, pooled_ref, cot_ref, bias_ref, grad_ref, first, second, deltas, sems):
    owners, rows, inner = first.shape
    half = rows // N_CORE
    copies = []
    for y in range(N_Y):
        for c in range(N_CORE):
            p = y * N_CORE + c
            copies.append(
                pltpu.make_async_copy(
                    pieces_ref.at[p, :, pl.ds(0, half), :],
                    first.at[:, pl.ds(c * half, half), pl.ds(y * 128, 128)],
                    sems.at[0, p],
                )
            )
            copies.append(
                pltpu.make_async_copy(
                    pieces_ref.at[p, :, pl.ds(half, 16), :],
                    second.at[:, pl.ds(c * half + (y % 2) * 16, 16), pl.ds((y // 2) * 128, 128)],
                    sems.at[1, p],
                )
            )
    for copy in copies:
        copy.start()
    for copy in copies:
        copy.wait()
    step = 256
    across = (((1,), (1,)), ((), ()))
    per = step // rows
    for k in range(inner // step):
        cols = slice(k * step, (k + 1) * step)
        columns = first[:, :, cols].reshape(owners * rows, step)
        units = second[k * per : (k + 1) * per].reshape(step, second.shape[2])
        hidden = jnp.dot(pooled_ref[...], columns, preferred_element_type=f32) + bias_ref[:, cols]
        back = lax.dot_general(cot_ref[...], units, across, preferred_element_type=f32)
        gate = jax.nn.sigmoid(hidden)
        deltas[:, cols] = (back * (gate * (1.0 + hidden * (1.0 - gate)))).astype(bf16)
    for k in range(owners * rows // step):
        features = first[k * per : (k + 1) * per].reshape(step, inner)
        grad_ref[:, k * step : (k + 1) * step] = lax.dot_general(
            deltas[...], features, across, preferred_element_type=f32
        ).astype(bf16)


def partial_body(counts_ref, grad_ref, out_ref):
    owners, tables, act, bags = counts_ref.shape
    emb = grad_ref.shape[1] // tables
    per = tables // N_CORE
    for t in range(tables):
        lookups = counts_ref[:, t, :, :].reshape(owners * act, bags)
        part = jnp.dot(lookups, grad_ref[:, t * emb : (t + 1) * emb], preferred_element_type=f32)
        at = (t % per) * emb
        out_ref[:, t // per, :, at : at + emb] = part.reshape(owners, act, emb).astype(bf16)


def clip_body(scale, limit, parts_ref, out_ref, rows):
    owners, cores, act, width = parts_ref.shape
    emb = rows.shape[1]
    for c in range(cores):
        total = parts_ref[0, c].astype(f32)
        for n in range(1, owners):
            total = total + parts_ref[n, c].astype(f32)
        total = total * scale
        for t in range(width // emb):
            grads = total[:, t * emb : (t + 1) * emb]
            norms = jnp.sqrt(jnp.sum(grads * grads, axis=-1, keepdims=True))
            clipped = grads * (limit / jnp.maximum(norms, limit))
            at = slice(t * act, (t + 1) * act)
            rows[at, :] = clipped if c == 0 else rows[at, :] + clipped
    both = rows[...].astype(bf16)
    for n in range(out_ref.shape[0]):
        out_ref[n] = both


def share_body(parts_ref, out_ref):
    total = parts_ref[0].astype(f32)
    for n in range(1, parts_ref.shape[0]):
        total = total + parts_ref[n].astype(f32)
    out_ref[...] = total


def update_body(core_ref, ids_ref, mine_ref, other_ref, table_ref, accum_ref, new_table_ref, new_accum_ref, dense):
    tables, act = ids_ref.shape
    per_core = tables // 2
    core = core_ref[0]
    dense[...] = jnp.zeros_like(dense)
    for ref, side in ((mine_ref, core), (other_ref, 1 - core)):
        for t in range(per_core):
            for a in range(act):
                table = side * per_core + t
                row = ids_ref[table, a]
                dense[table, pl.ds(row, 1), :] = ref[pl.ds(t * act + a, 1), :]
    for t in range(tables):
        summed = dense[t]
        new_acc = accum_ref[t] + summed * summed
        new_accum_ref[t] = new_acc
        new_table_ref[t] = table_ref[t] - learn_rate * summed / (jnp.sqrt(new_acc) + epsilon)


def shards(pooled, cotangent, w_first, b_first, w_second, counts, row_ids, table, accum):
    tables, act, bags = counts.shape
    emb = table.shape[2]
    samples = pooled.shape[0]
    inner, top = w_first.shape[1], w_second.shape[1]
    owners = lax.axis_size("narrow")
    scale = 1.0 / math.sqrt(bags)
    limit = clip_factor * math.sqrt(emb)
    wide = lax.axis_index("wide").astype(jnp.int32)
    core = jnp.bitwise_and(wide, N_CORE - 1)
    y = jnp.right_shift(wide, 2)
    core_at = core.reshape(1)
    half = w_first.shape[0] // N_CORE

    piece = call(
        piece_body,
        jax.ShapeDtypeStruct((owners, half + 16, 128), bf16),
        [SMEM, HBM, HBM],
        [pltpu.VMEM((half + 16, 128), bf16), pltpu.SemaphoreType.DMA((2,))],
        nbytes=MIB // 4,
        limit=2,
    )(jnp.stack([core, y]), w_first, w_second)
    spread = lax.all_to_all(piece, "narrow", 0, 0, tiled=True)
    by_owner = jnp.transpose(counts.reshape(tables, act, owners, samples), (2, 0, 1, 3))
    by_owner, spread = lax.optimization_barrier((by_owner, spread))
    pieces = lax.all_gather(spread, "wide", axis=0, axis_index_groups=YC_GROUPS)
    regrouped = lax.all_to_all(by_owner, "narrow", 0, 0, tiled=True)

    grad_in = call(
        tower_body,
        jax.ShapeDtypeStruct((samples, owners * w_first.shape[0]), bf16),
        [HBM] + [VMEM] * 3,
        [
            pltpu.VMEM((owners, w_first.shape[0], inner), bf16),
            pltpu.VMEM((owners, w_second.shape[0], top), bf16),
            pltpu.VMEM((samples, inner), bf16),
            pltpu.SemaphoreType.DMA((2, N_Y * N_CORE)),
        ],
        flops=2 * samples * inner * (2 * inner + top),
        nbytes=8 * MIB,
    )(pieces, pooled, cotangent, b_first.reshape(1, -1))

    parts = call(
        partial_body,
        jax.ShapeDtypeStruct((owners, N_CORE, act, tables // N_CORE * emb), bf16),
        [VMEM] * 2,
        flops=2 * owners * act * samples * tables * emb,
        nbytes=4 * MIB,
    )(regrouped, grad_in)
    arrived = lax.all_to_all(
        parts.reshape(owners * N_CORE, act, -1),
        ("wide", "narrow"),
        0,
        0,
        axis_index_groups=chip_pairs(owners),
        tiled=True,
    )

    half_rows = tables * act // N_CORE
    copies = call(
        functools.partial(clip_body, scale, limit),
        jax.ShapeDtypeStruct((N_Y * N_HI, half_rows, emb), bf16),
        [VMEM],
        [pltpu.VMEM((half_rows, emb), f32)],
        nbytes=MIB,
    )(arrived.reshape(parts.shape))
    shares = lax.all_to_all(copies, "wide", 0, 0, axis_index_groups=YZ_GROUPS, tiled=True)
    mine = call(share_body, jax.ShapeDtypeStruct((half_rows, emb), f32), [VMEM], nbytes=MIB)(shares)
    theirs = lax.ppermute(mine, "wide", CORE_SWAP)
    whole = jax.ShapeDtypeStruct(table.shape, f32)
    return call(
        update_body,
        (whole, whole),
        [SMEM, SMEM] + [VMEM] * 4,
        [pltpu.VMEM(table.shape, f32)],
        nbytes=2 * MIB,
    )(core_at, row_ids, mine, theirs, table, accum)


def solution(mesh):
    in_specs = (
        P(("wide", "narrow"), None),
        P(("wide", "narrow"), None),
        P("narrow", None),
        P(),
        P("narrow", None),
        P(None, "narrow", "wide"),
        P(None, "narrow"),
        P(None, "narrow", None),
        P(None, "narrow", None),
    )
    out_specs = (P(None, "narrow", None), P(None, "narrow", None))
    return jax.shard_map(shards, mesh=mesh, in_specs=in_specs, out_specs=out_specs, check_vma=False)
```

```python
import functools
import math

import jax
import jax.numpy as jnp
from jax import lax
from jax.experimental import pallas as pl
from jax.experimental.pallas import tpu as pltpu
from jax.sharding import PartitionSpec as P

clip_factor = 0.5
learn_rate = 0.05
epsilon = 1e-08

N_Y, N_HI, N_CORE = 8, 2, 2
bf16, f32 = jnp.bfloat16, jnp.float32
VMEM = pl.BlockSpec(memory_space=pltpu.VMEM)
SMEM = pl.BlockSpec(memory_space=pltpu.SMEM)
HBM = pl.BlockSpec(memory_space=pltpu.HBM)
MIB = 1 << 20


def wide_at(y, hi, core):
    return (y * N_HI + hi) * N_CORE + core


YZ_GROUPS = [[wide_at(y, h, c) for y in range(N_Y) for h in range(N_HI)] for c in range(N_CORE)]
CORE_SWAP = [(w, w ^ 1) for w in range(N_Y * N_HI * N_CORE)]
RING = [
    (wide_at(y, h, c), wide_at((y + 1 - 2 * c) % N_Y, h, c))
    for y in range(N_Y)
    for h in range(N_HI)
    for c in range(N_CORE)
]


def chip_pairs(owners):
    return [
        [wide_at(y, h, c) * owners + n for n in range(owners) for c in range(N_CORE)]
        for y in range(N_Y)
        for h in range(N_HI)
    ]


def call(body, out_shape, in_specs, scratch=(), flops=0, nbytes=0, limit=16):
    return pl.pallas_call(
        body,
        out_shape=out_shape,
        in_specs=in_specs,
        out_specs=jax.tree.map(lambda _: VMEM, out_shape),
        scratch_shapes=list(scratch),
        compiler_params=pltpu.CompilerParams(vmem_limit_bytes=limit * MIB),
        cost_estimate=pl.CostEstimate(flops=flops, bytes_accessed=nbytes, transcendentals=0),
    )


def piece_body(at_ref, first_ref, second_ref, out_ref, held, sems):
    core, y = at_ref[0], at_ref[1]
    half = first_ref.shape[0] // N_CORE
    top = pl.multiple_of(core * half, 32)
    low = pl.multiple_of(core * half + (y % 2) * 16, 16)
    copies = [
        pltpu.make_async_copy(
            first_ref.at[pl.ds(top, half), pl.ds(pl.multiple_of(y * 128, 128), 128)],
            held.at[pl.ds(0, half), :],
            sems.at[0],
        ),
        pltpu.make_async_copy(
            second_ref.at[pl.ds(low, 16), pl.ds(pl.multiple_of((y // 2) * 128, 128), 128)],
            held.at[pl.ds(half, 16), :],
            sems.at[1],
        ),
    ]
    for copy in copies:
        copy.start()
    for copy in copies:
        copy.wait()
    for n in range(out_ref.shape[0]):
        out_ref[n] = held[...]


def tower_body(at_ref, *refs):
    pieces, (pooled_ref, cot_ref, bias_ref, grad_ref, first, second, deltas, sems) = refs[:9], refs[9:]
    core, y = at_ref[0], at_ref[1]
    owners, rows, inner = first.shape
    half = rows // N_CORE
    whole, ahead, swapped = pieces[0], pieces[1:5], pieces[5:9]
    blocks = [(whole.at[0], 0, core), (whole.at[1], 0, 1 - core)]
    for k in range(1, 4):
        for part in range(N_CORE):
            blocks.append((ahead[k - 1].at[part], (2 * core - 1) * k, core if part == 0 else 1 - core))
            blocks.append((swapped[k - 1].at[part], (1 - 2 * core) * k, 1 - core if part == 0 else core))
    blocks.append((ahead[3], 4, core))
    blocks.append((swapped[3], 4, 1 - core))
    copies = []
    for p, (ref, shift, side) in enumerate(blocks):
        source = jnp.bitwise_and(y + shift + N_Y, N_Y - 1)
        top = pl.multiple_of(side * half, 32)
        low = pl.multiple_of(side * half + jnp.bitwise_and(source, 1) * 16, 16)
        units = pl.multiple_of(source * 128, 128)
        tops = pl.multiple_of(jnp.right_shift(source, 1) * 128, 128)
        copies.append(
            pltpu.make_async_copy(
                ref.at[:, pl.ds(0, half), :], first.at[:, pl.ds(top, half), pl.ds(units, 128)], sems.at[0, p]
            )
        )
        copies.append(
            pltpu.make_async_copy(
                ref.at[:, pl.ds(half, 16), :], second.at[:, pl.ds(low, 16), pl.ds(tops, 128)], sems.at[1, p]
            )
        )
    for copy in copies:
        copy.start()
    for copy in copies:
        copy.wait()
    step = 256
    across = (((1,), (1,)), ((), ()))
    per = step // rows
    for k in range(inner // step):
        cols = slice(k * step, (k + 1) * step)
        columns = first[:, :, cols].reshape(owners * rows, step)
        units = second[k * per : (k + 1) * per].reshape(step, second.shape[2])
        hidden = jnp.dot(pooled_ref[...], columns, preferred_element_type=f32) + bias_ref[:, cols]
        back = lax.dot_general(cot_ref[...], units, across, preferred_element_type=f32)
        gate = jax.nn.sigmoid(hidden)
        deltas[:, cols] = (back * (gate * (1.0 + hidden * (1.0 - gate)))).astype(bf16)
    for k in range(owners * rows // step):
        features = first[k * per : (k + 1) * per].reshape(step, inner)
        grad_ref[:, k * step : (k + 1) * step] = lax.dot_general(
            deltas[...], features, across, preferred_element_type=f32
        ).astype(bf16)


def partial_body(counts_ref, grad_ref, out_ref):
    owners, tables, act, bags = counts_ref.shape
    emb = grad_ref.shape[1] // tables
    per = tables // N_CORE
    for t in range(tables):
        lookups = counts_ref[:, t, :, :].reshape(owners * act, bags)
        part = jnp.dot(lookups, grad_ref[:, t * emb : (t + 1) * emb], preferred_element_type=f32)
        at = (t % per) * emb
        out_ref[:, t // per, :, at : at + emb] = part.reshape(owners, act, emb).astype(bf16)


def clip_body(scale, limit, parts_ref, out_ref, rows):
    owners, cores, act, width = parts_ref.shape
    emb = rows.shape[1]
    for c in range(cores):
        total = parts_ref[0, c].astype(f32)
        for n in range(1, owners):
            total = total + parts_ref[n, c].astype(f32)
        total = total * scale
        for t in range(width // emb):
            grads = total[:, t * emb : (t + 1) * emb]
            norms = jnp.sqrt(jnp.sum(grads * grads, axis=-1, keepdims=True))
            clipped = grads * (limit / jnp.maximum(norms, limit))
            at = slice(t * act, (t + 1) * act)
            rows[at, :] = clipped if c == 0 else rows[at, :] + clipped
    both = rows[...].astype(bf16)
    for n in range(out_ref.shape[0]):
        out_ref[n] = both


def share_body(parts_ref, out_ref):
    total = parts_ref[0].astype(f32)
    for n in range(1, parts_ref.shape[0]):
        total = total + parts_ref[n].astype(f32)
    out_ref[...] = total


def update_body(core_ref, ids_ref, mine_ref, other_ref, table_ref, accum_ref, new_table_ref, new_accum_ref, dense):
    tables, act = ids_ref.shape
    per_core = tables // 2
    core = core_ref[0]
    dense[...] = jnp.zeros_like(dense)
    for ref, side in ((mine_ref, core), (other_ref, 1 - core)):
        for t in range(per_core):
            for a in range(act):
                table = side * per_core + t
                row = ids_ref[table, a]
                dense[table, pl.ds(row, 1), :] = ref[pl.ds(t * act + a, 1), :]
    for t in range(tables):
        summed = dense[t]
        new_acc = accum_ref[t] + summed * summed
        new_accum_ref[t] = new_acc
        new_table_ref[t] = table_ref[t] - learn_rate * summed / (jnp.sqrt(new_acc) + epsilon)


def shards(pooled, cotangent, w_first, b_first, w_second, counts, row_ids, table, accum):
    tables, act, bags = counts.shape
    emb = table.shape[2]
    samples = pooled.shape[0]
    inner, top = w_first.shape[1], w_second.shape[1]
    owners = lax.axis_size("narrow")
    scale = 1.0 / math.sqrt(bags)
    limit = clip_factor * math.sqrt(emb)
    wide = lax.axis_index("wide").astype(jnp.int32)
    core = jnp.bitwise_and(wide, N_CORE - 1)
    y = jnp.right_shift(wide, 2)
    core_at = core.reshape(1)
    half = w_first.shape[0] // N_CORE

    place = jnp.stack([core, y])
    piece = call(
        piece_body,
        jax.ShapeDtypeStruct((owners, half + 16, 128), bf16),
        [SMEM, HBM, HBM],
        [pltpu.VMEM((half + 16, 128), bf16), pltpu.SemaphoreType.DMA((2,))],
        nbytes=MIB // 4,
        limit=2,
    )(place, w_first, w_second)
    spread = lax.all_to_all(piece, "narrow", 0, 0, tiled=True)
    by_owner = jnp.transpose(counts.reshape(tables, act, owners, samples), (2, 0, 1, 3))
    by_owner, spread = lax.optimization_barrier((by_owner, spread))
    regrouped = lax.all_to_all(by_owner, "narrow", 0, 0, tiled=True)

    ring = [jnp.stack([spread, lax.ppermute(spread, "wide", CORE_SWAP)])]
    swapped = []
    for k in range(1, 5):
        sent = ring[-1] if k < 4 else ring[-1][0]
        ring.append(lax.ppermute(sent, "wide", RING))
        swapped.append(lax.ppermute(ring[-1], "wide", CORE_SWAP))

    grad_in = call(
        tower_body,
        jax.ShapeDtypeStruct((samples, owners * w_first.shape[0]), bf16),
        [SMEM] + [HBM] * 9 + [VMEM] * 3,
        [
            pltpu.VMEM((owners, w_first.shape[0], inner), bf16),
            pltpu.VMEM((owners, w_second.shape[0], top), bf16),
            pltpu.VMEM((samples, inner), bf16),
            pltpu.SemaphoreType.DMA((2, N_Y * N_CORE)),
        ],
        flops=2 * samples * inner * (2 * inner + top),
        nbytes=8 * MIB,
    )(place, *ring, *swapped, pooled, cotangent, b_first.reshape(1, -1))

    parts = call(
        partial_body,
        jax.ShapeDtypeStruct((owners, N_CORE, act, tables // N_CORE * emb), bf16),
        [VMEM] * 2,
        flops=2 * owners * act * samples * tables * emb,
        nbytes=4 * MIB,
    )(regrouped, grad_in)
    arrived = lax.all_to_all(
        parts.reshape(owners * N_CORE, act, -1),
        ("wide", "narrow"),
        0,
        0,
        axis_index_groups=chip_pairs(owners),
        tiled=True,
    )

    half_rows = tables * act // N_CORE
    copies = call(
        functools.partial(clip_body, scale, limit),
        jax.ShapeDtypeStruct((N_Y * N_HI, half_rows, emb), bf16),
        [VMEM],
        [pltpu.VMEM((half_rows, emb), f32)],
        nbytes=MIB,
    )(arrived.reshape(parts.shape))
    shares = lax.all_to_all(copies, "wide", 0, 0, axis_index_groups=YZ_GROUPS, tiled=True)
    mine = call(share_body, jax.ShapeDtypeStruct((half_rows, emb), f32), [VMEM], nbytes=MIB)(shares)
    theirs = lax.ppermute(mine, "wide", CORE_SWAP)
    whole = jax.ShapeDtypeStruct(table.shape, f32)
    return call(
        update_body,
        (whole, whole),
        [SMEM, SMEM] + [VMEM] * 4,
        [pltpu.VMEM(table.shape, f32)],
        nbytes=2 * MIB,
    )(core_at, row_ids, mine, theirs, table, accum)


def solution(mesh):
    in_specs = (
        P(("wide", "narrow"), None),
        P(("wide", "narrow"), None),
        P("narrow", None),
        P(),
        P("narrow", None),
        P(None, "narrow", "wide"),
        P(None, "narrow"),
        P(None, "narrow", None),
        P(None, "narrow", None),
    )
    out_specs = (P(None, "narrow", None), P(None, "narrow", None))
    return jax.shard_map(shards, mesh=mesh, in_specs=in_specs, out_specs=out_specs, check_vma=False)
```

```python
import functools
import math

import jax
import jax.numpy as jnp
from jax import lax
from jax.experimental import pallas as pl
from jax.experimental.pallas import tpu as pltpu
from jax.sharding import PartitionSpec as P

clip_factor = 0.5
learn_rate = 0.05
epsilon = 1e-08

N_Y, N_HI, N_CORE = 8, 2, 2
bf16, f32 = jnp.bfloat16, jnp.float32
VMEM = pl.BlockSpec(memory_space=pltpu.VMEM)
SMEM = pl.BlockSpec(memory_space=pltpu.SMEM)
HBM = pl.BlockSpec(memory_space=pltpu.HBM)
MIB = 1 << 20


def wide_at(y, hi, core):
    return (y * N_HI + hi) * N_CORE + core


YZ_GROUPS = [[wide_at(y, h, c) for y in range(N_Y) for h in range(N_HI)] for c in range(N_CORE)]
CORE_SWAP = [(w, w ^ 1) for w in range(N_Y * N_HI * N_CORE)]


def y_shift(by):
    return [
        (wide_at(y, h, c), wide_at((y + by - 2 * by * c) % N_Y, h, c))
        for y in range(N_Y)
        for h in range(N_HI)
        for c in range(N_CORE)
    ]


def in_hbm(x):
    return pltpu.with_memory_space_constraint(x, pltpu.HBM)


def chip_pairs(owners):
    return [
        [wide_at(y, h, c) * owners + n for n in range(owners) for c in range(N_CORE)]
        for y in range(N_Y)
        for h in range(N_HI)
    ]


def call(body, out_shape, in_specs, scratch=(), flops=0, nbytes=0, limit=16):
    return pl.pallas_call(
        body,
        out_shape=out_shape,
        in_specs=in_specs,
        out_specs=jax.tree.map(lambda _: VMEM, out_shape),
        scratch_shapes=list(scratch),
        compiler_params=pltpu.CompilerParams(vmem_limit_bytes=limit * MIB),
        cost_estimate=pl.CostEstimate(flops=flops, bytes_accessed=nbytes, transcendentals=0),
    )


def piece_body(at_ref, first_ref, second_ref, out_ref, held, sems):
    core, y = at_ref[0], at_ref[1]
    half = first_ref.shape[0] // N_CORE
    top = pl.multiple_of(core * half, 32)
    low = pl.multiple_of(core * half + (y % 2) * 16, 16)
    copies = [
        pltpu.make_async_copy(
            first_ref.at[pl.ds(top, half), pl.ds(pl.multiple_of(y * 128, 128), 128)],
            held.at[pl.ds(0, half), :],
            sems.at[0],
        ),
        pltpu.make_async_copy(
            second_ref.at[pl.ds(low, 16), pl.ds(pl.multiple_of((y // 2) * 128, 128), 128)],
            held.at[pl.ds(half, 16), :],
            sems.at[1],
        ),
    ]
    for copy in copies:
        copy.start()
    for copy in copies:
        copy.wait()
    for n in range(out_ref.shape[0]):
        out_ref[n] = held[...]


def tower_body(at_ref, *refs):
    pieces = refs[:9]
    pooled_hbm, cot_hbm, bias_ref, grad_ref, first, second, deltas, pooled_ref, cot_ref, sems = refs[9:]
    core, y = at_ref[0], at_ref[1]
    owners, rows, inner = first.shape
    half = rows // N_CORE
    whole, ahead, swapped = pieces[0], pieces[1:5], pieces[5:9]
    blocks = [(whole.at[0], 0, core), (whole.at[1], 0, 1 - core)]
    for k in range(1, 4):
        for part in range(N_CORE):
            blocks.append((ahead[k - 1].at[part], (2 * core - 1) * k, core if part == 0 else 1 - core))
            blocks.append((swapped[k - 1].at[part], (1 - 2 * core) * k, 1 - core if part == 0 else core))
    blocks.append((ahead[3], 4, core))
    blocks.append((swapped[3], 4, 1 - core))
    copies = [
        pltpu.make_async_copy(pooled_hbm, pooled_ref, sems.at[0, len(blocks)]),
        pltpu.make_async_copy(cot_hbm, cot_ref, sems.at[1, len(blocks)]),
    ]
    for p, (ref, shift, side) in enumerate(blocks):
        source = jnp.bitwise_and(y + shift + N_Y, N_Y - 1)
        top = pl.multiple_of(side * half, 32)
        low = pl.multiple_of(side * half + jnp.bitwise_and(source, 1) * 16, 16)
        units = pl.multiple_of(source * 128, 128)
        tops = pl.multiple_of(jnp.right_shift(source, 1) * 128, 128)
        copies.append(
            pltpu.make_async_copy(
                ref.at[:, pl.ds(0, half), :], first.at[:, pl.ds(top, half), pl.ds(units, 128)], sems.at[0, p]
            )
        )
        copies.append(
            pltpu.make_async_copy(
                ref.at[:, pl.ds(half, 16), :], second.at[:, pl.ds(low, 16), pl.ds(tops, 128)], sems.at[1, p]
            )
        )
    for copy in copies:
        copy.start()
    for copy in copies:
        copy.wait()
    step = 256
    across = (((1,), (1,)), ((), ()))
    per = step // rows
    for k in range(inner // step):
        cols = slice(k * step, (k + 1) * step)
        columns = first[:, :, cols].reshape(owners * rows, step)
        units = second[k * per : (k + 1) * per].reshape(step, second.shape[2])
        hidden = jnp.dot(pooled_ref[...], columns, preferred_element_type=f32) + bias_ref[:, cols]
        back = lax.dot_general(cot_ref[...], units, across, preferred_element_type=f32)
        gate = jax.nn.sigmoid(hidden)
        deltas[:, cols] = (back * (gate * (1.0 + hidden * (1.0 - gate)))).astype(bf16)
    for k in range(owners * rows // step):
        features = first[k * per : (k + 1) * per].reshape(step, inner)
        grad_ref[:, k * step : (k + 1) * step] = lax.dot_general(
            deltas[...], features, across, preferred_element_type=f32
        ).astype(bf16)


def partial_body(counts_ref, grad_ref, out_ref):
    owners, tables, act, bags = counts_ref.shape
    emb = grad_ref.shape[1] // tables
    per = tables // N_CORE
    for t in range(tables):
        lookups = counts_ref[:, t, :, :].reshape(owners * act, bags)
        part = jnp.dot(lookups, grad_ref[:, t * emb : (t + 1) * emb], preferred_element_type=f32)
        at = (t % per) * emb
        out_ref[:, t // per, :, at : at + emb] = part.reshape(owners, act, emb).astype(bf16)


def clip_body(scale, limit, parts_ref, out_ref, rows):
    owners, cores, act, width = parts_ref.shape
    emb = rows.shape[1]
    for c in range(cores):
        total = parts_ref[0, c].astype(f32)
        for n in range(1, owners):
            total = total + parts_ref[n, c].astype(f32)
        total = total * scale
        for t in range(width // emb):
            grads = total[:, t * emb : (t + 1) * emb]
            norms = jnp.sqrt(jnp.sum(grads * grads, axis=-1, keepdims=True))
            clipped = grads * (limit / jnp.maximum(norms, limit))
            at = slice(t * act, (t + 1) * act)
            rows[at, :] = clipped if c == 0 else rows[at, :] + clipped
    both = rows[...].astype(bf16)
    for n in range(out_ref.shape[0]):
        out_ref[n] = both


def share_body(parts_ref, out_ref):
    total = parts_ref[0].astype(f32)
    for n in range(1, parts_ref.shape[0]):
        total = total + parts_ref[n].astype(f32)
    out_ref[...] = total


def update_body(core_ref, ids_ref, mine_ref, other_ref, table_ref, accum_ref, new_table_ref, new_accum_ref, dense):
    tables, act = ids_ref.shape
    per_core = tables // 2
    core = core_ref[0]
    dense[...] = jnp.zeros_like(dense)
    for ref, side in ((mine_ref, core), (other_ref, 1 - core)):
        for t in range(per_core):
            for a in range(act):
                table = side * per_core + t
                row = ids_ref[table, a]
                dense[table, pl.ds(row, 1), :] = ref[pl.ds(t * act + a, 1), :]
    for t in range(tables):
        summed = dense[t]
        new_acc = accum_ref[t] + summed * summed
        new_accum_ref[t] = new_acc
        new_table_ref[t] = table_ref[t] - learn_rate * summed / (jnp.sqrt(new_acc) + epsilon)


def shards(pooled, cotangent, w_first, b_first, w_second, counts, row_ids, table, accum):
    tables, act, bags = counts.shape
    emb = table.shape[2]
    samples = pooled.shape[0]
    inner, top = w_first.shape[1], w_second.shape[1]
    owners = lax.axis_size("narrow")
    scale = 1.0 / math.sqrt(bags)
    limit = clip_factor * math.sqrt(emb)
    wide = lax.axis_index("wide").astype(jnp.int32)
    core = jnp.bitwise_and(wide, N_CORE - 1)
    y = jnp.right_shift(wide, 2)
    core_at = core.reshape(1)
    half = w_first.shape[0] // N_CORE

    place = jnp.stack([core, y])
    piece = call(
        piece_body,
        jax.ShapeDtypeStruct((owners, half + 16, 128), bf16),
        [SMEM, HBM, HBM],
        [pltpu.VMEM((half + 16, 128), bf16), pltpu.SemaphoreType.DMA((2,))],
        nbytes=MIB // 4,
        limit=2,
    )(place, in_hbm(w_first), in_hbm(w_second))
    spread = lax.all_to_all(piece, "narrow", 0, 0, tiled=True)
    by_owner = jnp.transpose(counts.reshape(tables, act, owners, samples), (2, 0, 1, 3))
    by_owner, spread = lax.optimization_barrier((by_owner, spread))
    regrouped = lax.all_to_all(by_owner, "narrow", 0, 0, tiled=True)

    whole = jnp.stack([spread, lax.ppermute(spread, "wide", CORE_SWAP)])
    ahead2 = lax.ppermute(whole, "wide", y_shift(2))
    ahead1 = lax.ppermute(whole, "wide", y_shift(1))
    ahead3 = lax.ppermute(ahead2, "wide", y_shift(1))
    ahead4 = lax.ppermute(ahead2[0], "wide", y_shift(2))
    ring = [ahead1, ahead2, ahead3, ahead4]
    swapped = [lax.ppermute(block, "wide", CORE_SWAP) for block in ring]

    grad_in = call(
        tower_body,
        jax.ShapeDtypeStruct((samples, owners * w_first.shape[0]), bf16),
        [SMEM] + [HBM] * 11 + [VMEM],
        [
            pltpu.VMEM((owners, w_first.shape[0], inner), bf16),
            pltpu.VMEM((owners, w_second.shape[0], top), bf16),
            pltpu.VMEM((samples, inner), bf16),
            pltpu.VMEM(pooled.shape, bf16),
            pltpu.VMEM(cotangent.shape, bf16),
            pltpu.SemaphoreType.DMA((2, N_Y * N_CORE + 1)),
        ],
        flops=2 * samples * inner * (2 * inner + top),
        nbytes=8 * MIB,
    )(place, whole, *ring, *swapped, in_hbm(pooled), in_hbm(cotangent), b_first.reshape(1, -1))

    parts = call(
        partial_body,
        jax.ShapeDtypeStruct((owners, N_CORE, act, tables // N_CORE * emb), bf16),
        [VMEM] * 2,
        flops=2 * owners * act * samples * tables * emb,
        nbytes=4 * MIB,
    )(regrouped, grad_in)
    arrived = lax.all_to_all(
        parts.reshape(owners * N_CORE, act, -1),
        ("wide", "narrow"),
        0,
        0,
        axis_index_groups=chip_pairs(owners),
        tiled=True,
    )

    half_rows = tables * act // N_CORE
    copies = call(
        functools.partial(clip_body, scale, limit),
        jax.ShapeDtypeStruct((N_Y * N_HI, half_rows, emb), bf16),
        [VMEM],
        [pltpu.VMEM((half_rows, emb), f32)],
        nbytes=MIB,
    )(arrived.reshape(parts.shape))
    shares = lax.all_to_all(copies, "wide", 0, 0, axis_index_groups=YZ_GROUPS, tiled=True)
    mine = call(share_body, jax.ShapeDtypeStruct((half_rows, emb), f32), [VMEM], nbytes=MIB)(shares)
    theirs = lax.ppermute(mine, "wide", CORE_SWAP)
    whole = jax.ShapeDtypeStruct(table.shape, f32)
    return call(
        update_body,
        (whole, whole),
        [SMEM, SMEM] + [VMEM] * 4,
        [pltpu.VMEM(table.shape, f32)],
        nbytes=2 * MIB,
    )(core_at, row_ids, mine, theirs, table, accum)


def solution(mesh):
    in_specs = (
        P(("wide", "narrow"), None),
        P(("wide", "narrow"), None),
        P("narrow", None),
        P(),
        P("narrow", None),
        P(None, "narrow", "wide"),
        P(None, "narrow"),
        P(None, "narrow", None),
        P(None, "narrow", None),
    )
    out_specs = (P(None, "narrow", None), P(None, "narrow", None))
    return jax.shard_map(shards, mesh=mesh, in_specs=in_specs, out_specs=out_specs, check_vma=False)
```

```python
import functools
import math

import jax
import jax.numpy as jnp
from jax import lax
from jax.experimental import pallas as pl
from jax.experimental.pallas import tpu as pltpu
from jax.sharding import PartitionSpec as P

clip_factor = 0.5
learn_rate = 0.05
epsilon = 1e-08

N_Y, N_HI, N_CORE = 8, 2, 2
bf16, f32 = jnp.bfloat16, jnp.float32
VMEM = pl.BlockSpec(memory_space=pltpu.VMEM)
SMEM = pl.BlockSpec(memory_space=pltpu.SMEM)
HBM = pl.BlockSpec(memory_space=pltpu.HBM)
MIB = 1 << 20


def wide_at(y, hi, core):
    return (y * N_HI + hi) * N_CORE + core


CORE_SWAP = [(w, w ^ 1) for w in range(N_Y * N_HI * N_CORE)]


def y_shift(by):
    return [
        (wide_at(y, h, c), wide_at((y + by - 2 * by * c) % N_Y, h, c))
        for y in range(N_Y)
        for h in range(N_HI)
        for c in range(N_CORE)
    ]


def in_hbm(x):
    return pltpu.with_memory_space_constraint(x, pltpu.HBM)


def quads(owners):
    return [
        [wide_at(y, h, c) * owners + n for c in range(N_CORE) for h in range(N_HI) for n in range(owners)]
        for y in range(N_Y)
    ]


WIDE_ORDER = [
    [wide_at(y, h, c) for c in range(N_CORE) for h in range(N_HI) for y in range(N_Y)]
]
N_X = 4


def offset_of(y, core):
    return 2 * (1 - core) if y < 4 else 1 + 2 * core, y % N_X


def shard_moves(owners):
    n_z = owners // N_X
    moves = []
    for y in range(N_Y):
        for h in range(N_HI):
            for c in range(N_CORE):
                dz, dx = offset_of(y, c)
                for z in range(n_z):
                    for x in range(N_X):
                        to = (z + dz) % n_z * N_X + (x + dx) % N_X
                        base = wide_at(y, h, c) * owners
                        moves.append((base + z * N_X + x, base + to))
    return moves


def call(body, out_shape, in_specs, scratch=(), flops=0, nbytes=0, limit=16):
    return pl.pallas_call(
        body,
        out_shape=out_shape,
        in_specs=in_specs,
        out_specs=jax.tree.map(lambda _: VMEM, out_shape),
        scratch_shapes=list(scratch),
        compiler_params=pltpu.CompilerParams(vmem_limit_bytes=limit * MIB),
        cost_estimate=pl.CostEstimate(flops=flops, bytes_accessed=nbytes, transcendentals=0),
    )


def join_body(first_ref, second_ref, out_ref, sems):
    inner = first_ref.shape[1]
    copies = [
        pltpu.make_async_copy(first_ref, out_ref.at[:, pl.ds(0, inner)], sems.at[0]),
        pltpu.make_async_copy(second_ref, out_ref.at[:, pl.ds(inner, second_ref.shape[1])], sems.at[1]),
    ]
    for copy in copies:
        copy.start()
    for copy in copies:
        copy.wait()


def tower_body(at_ref, *refs):
    whole, ahead, swapped = refs[0], refs[1:5], refs[5:9]
    pooled_hbm, cot_hbm, bias_ref, grad_ref, first, second, deltas, pooled_ref, cot_ref, sems = refs[9:]
    core, y, z, x = at_ref[0], at_ref[1], at_ref[2], at_ref[3]
    owners, rows, inner = first.shape
    top = second.shape[2]
    blocks = [(whole.at[0], 0, core), (whole.at[1], 0, 1 - core)]
    for k in range(1, 4):
        for part in range(N_CORE):
            blocks.append((ahead[k - 1].at[part], (2 * core - 1) * k, core if part == 0 else 1 - core))
            blocks.append((swapped[k - 1].at[part], (1 - 2 * core) * k, 1 - core if part == 0 else core))
    blocks.append((ahead[3], 4, core))
    blocks.append((swapped[3], 4, 1 - core))
    copies = [
        pltpu.make_async_copy(pooled_hbm, pooled_ref, sems.at[0, len(blocks)]),
        pltpu.make_async_copy(cot_hbm, cot_ref, sems.at[1, len(blocks)]),
    ]
    for p, (ref, shift, side) in enumerate(blocks):
        source = jnp.bitwise_and(y + shift + N_Y, N_Y - 1)
        dz = jnp.where(source < 4, 2 * (1 - side), 1 + 2 * side)
        from_z = jnp.bitwise_and(z - dz + 4, owners // N_X - 1)
        from_x = jnp.bitwise_and(x - source + N_Y, N_X - 1)
        owner = from_z * N_X + from_x
        copies.append(pltpu.make_async_copy(ref.at[:, pl.ds(0, inner)], first.at[owner], sems.at[0, p]))
        copies.append(pltpu.make_async_copy(ref.at[:, pl.ds(inner, top)], second.at[owner], sems.at[1, p]))
    for copy in copies:
        copy.start()
    for copy in copies:
        copy.wait()
    step = 256
    across = (((1,), (1,)), ((), ()))
    per = step // rows
    for k in range(inner // step):
        cols = slice(k * step, (k + 1) * step)
        columns = first[:, :, cols].reshape(owners * rows, step)
        units = second[k * per : (k + 1) * per].reshape(step, second.shape[2])
        hidden = jnp.dot(pooled_ref[...], columns, preferred_element_type=f32) + bias_ref[:, cols]
        back = lax.dot_general(cot_ref[...], units, across, preferred_element_type=f32)
        gate = jax.nn.sigmoid(hidden)
        deltas[:, cols] = (back * (gate * (1.0 + hidden * (1.0 - gate)))).astype(bf16)
    for k in range(owners * rows // step):
        features = first[k * per : (k + 1) * per].reshape(step, inner)
        grad_ref[:, k * step : (k + 1) * step] = lax.dot_general(
            deltas[...], features, across, preferred_element_type=f32
        ).astype(bf16)


def partial_body(counts_ref, grad_ref, out_ref):
    owners, tables, act, bags = counts_ref.shape
    emb = grad_ref.shape[1] // tables
    per = tables // out_ref.shape[0]
    for t in range(tables):
        lookups = counts_ref[:, t, :, :].reshape(owners * act, bags)
        part = jnp.dot(lookups, grad_ref[:, t * emb : (t + 1) * emb], preferred_element_type=f32)
        at = (t % per) * emb
        out_ref[t // per, :, :, at : at + emb] = part.reshape(owners, act, emb).astype(bf16)


def clip_body(scale, limit, parts_ref, out_ref, rows):
    groups, owners, act, width = parts_ref.shape
    emb = rows.shape[1]
    for g in range(groups):
        total = parts_ref[g, 0].astype(f32)
        for n in range(1, owners):
            total = total + parts_ref[g, n].astype(f32)
        total = total * scale
        for t in range(width // emb):
            grads = total[:, t * emb : (t + 1) * emb]
            norms = jnp.sqrt(jnp.sum(grads * grads, axis=-1, keepdims=True))
            clipped = grads * (limit / jnp.maximum(norms, limit))
            at = slice(t * act, (t + 1) * act)
            rows[at, :] = clipped if g == 0 else rows[at, :] + clipped
    both = rows[...].astype(bf16)
    for n in range(out_ref.shape[0]):
        out_ref[n] = both


def update_body(ids_ref, shares_ref, table_ref, accum_ref, new_table_ref, new_accum_ref, dense, rows):
    tables, act = ids_ref.shape
    quarters = N_HI * N_CORE
    per = tables // quarters
    dense[...] = jnp.zeros_like(dense)
    for q in range(quarters):
        total = shares_ref[q * N_Y].astype(f32)
        for y in range(1, N_Y):
            total = total + shares_ref[q * N_Y + y].astype(f32)
        rows[...] = total
        for t in range(per):
            table = q * per + t
            for a in range(act):
                row = ids_ref[table, a]
                dense[table, pl.ds(row, 1), :] = rows[pl.ds(t * act + a, 1), :]
    for t in range(tables):
        summed = dense[t]
        new_acc = accum_ref[t] + summed * summed
        new_accum_ref[t] = new_acc
        new_table_ref[t] = table_ref[t] - learn_rate * summed / (jnp.sqrt(new_acc) + epsilon)


def shards(pooled, cotangent, w_first, b_first, w_second, counts, row_ids, table, accum):
    tables, act, bags = counts.shape
    emb = table.shape[2]
    samples = pooled.shape[0]
    inner, top = w_first.shape[1], w_second.shape[1]
    owners = lax.axis_size("narrow")
    scale = 1.0 / math.sqrt(bags)
    limit = clip_factor * math.sqrt(emb)
    wide = lax.axis_index("wide").astype(jnp.int32)
    core = jnp.bitwise_and(wide, N_CORE - 1)
    y = jnp.right_shift(wide, 2)
    narrow = lax.axis_index("narrow").astype(jnp.int32)
    place = jnp.stack([core, y, jnp.right_shift(narrow, 2), jnp.bitwise_and(narrow, N_X - 1)])

    shard = call(
        join_body,
        jax.ShapeDtypeStruct((w_first.shape[0], inner + top), bf16),
        [HBM, HBM],
        [pltpu.SemaphoreType.DMA((2,))],
        nbytes=MIB // 2,
        limit=2,
    )(in_hbm(w_first), in_hbm(w_second))
    moved = lax.ppermute(shard, ("wide", "narrow"), shard_moves(owners))
    by_owner = jnp.transpose(counts.reshape(tables, act, owners, samples), (2, 0, 1, 3))
    by_owner, moved = lax.optimization_barrier((by_owner, moved))
    regrouped = lax.all_to_all(by_owner, "narrow", 0, 0, tiled=True)
    whole = jnp.stack([moved, lax.ppermute(moved, "wide", CORE_SWAP)])
    ahead2 = lax.ppermute(whole, "wide", y_shift(2))
    ahead1 = lax.ppermute(whole, "wide", y_shift(1))
    ahead3 = lax.ppermute(ahead2, "wide", y_shift(1))
    ahead4 = lax.ppermute(ahead2[0], "wide", y_shift(2))
    ring = [ahead1, ahead2, ahead3, ahead4]
    swapped = [lax.ppermute(block, "wide", CORE_SWAP) for block in ring]

    grad_in = call(
        tower_body,
        jax.ShapeDtypeStruct((samples, owners * w_first.shape[0]), bf16),
        [SMEM] + [HBM] * 11 + [VMEM],
        [
            pltpu.VMEM((owners, w_first.shape[0], inner), bf16),
            pltpu.VMEM((owners, w_second.shape[0], top), bf16),
            pltpu.VMEM((samples, inner), bf16),
            pltpu.VMEM(pooled.shape, bf16),
            pltpu.VMEM(cotangent.shape, bf16),
            pltpu.SemaphoreType.DMA((2, N_Y * N_CORE + 1)),
        ],
        flops=2 * samples * inner * (2 * inner + top),
        nbytes=8 * MIB,
    )(place, *map(in_hbm, (whole, *ring, *swapped, pooled, cotangent)), b_first.reshape(1, -1))

    quarters = N_HI * N_CORE
    parts = call(
        partial_body,
        jax.ShapeDtypeStruct((quarters, owners, act, tables // quarters * emb), bf16),
        [VMEM] * 2,
        flops=2 * owners * act * samples * tables * emb,
        nbytes=4 * MIB,
    )(regrouped, grad_in)
    arrived = lax.all_to_all(
        parts.reshape(owners * quarters, act, -1),
        ("wide", "narrow"),
        0,
        0,
        axis_index_groups=quads(owners),
        tiled=True,
    )
    rows = tables * act // quarters
    copies = call(
        functools.partial(clip_body, scale, limit),
        jax.ShapeDtypeStruct((N_Y * quarters, rows, emb), bf16),
        [VMEM],
        [pltpu.VMEM((rows, emb), f32)],
        nbytes=MIB,
    )(arrived.reshape(parts.shape))
    shares = lax.all_to_all(copies, "wide", 0, 0, axis_index_groups=WIDE_ORDER, tiled=True)
    updated = jax.ShapeDtypeStruct(table.shape, f32)
    return call(
        update_body,
        (updated, updated),
        [SMEM] + [VMEM] * 3,
        [pltpu.VMEM(table.shape, f32), pltpu.VMEM((rows, emb), f32)],
        nbytes=2 * MIB,
    )(row_ids, shares, table, accum)


def solution(mesh):
    in_specs = (
        P(("wide", "narrow"), None),
        P(("wide", "narrow"), None),
        P("narrow", None),
        P(),
        P("narrow", None),
        P(None, "narrow", "wide"),
        P(None, "narrow"),
        P(None, "narrow", None),
        P(None, "narrow", None),
    )
    out_specs = (P(None, "narrow", None), P(None, "narrow", None))
    return jax.shard_map(shards, mesh=mesh, in_specs=in_specs, out_specs=out_specs, check_vma=False)
```

```python
import functools
import math

import jax
import jax.numpy as jnp
from jax import lax
from jax.experimental import pallas as pl
from jax.experimental.pallas import tpu as pltpu
from jax.sharding import PartitionSpec as P

clip_factor = 0.5
learn_rate = 0.05
epsilon = 1e-08

N_Y, N_HI, N_CORE = 8, 2, 2
bf16, f32 = jnp.bfloat16, jnp.float32
VMEM = pl.BlockSpec(memory_space=pltpu.VMEM)
SMEM = pl.BlockSpec(memory_space=pltpu.SMEM)
HBM = pl.BlockSpec(memory_space=pltpu.HBM)
MIB = 1 << 20


def wide_at(y, hi, core):
    return (y * N_HI + hi) * N_CORE + core


CORE_SWAP = [(w, w ^ 1) for w in range(N_Y * N_HI * N_CORE)]


def y_shift(by):
    return [
        (wide_at(y, h, c), wide_at((y + by - 2 * by * c) % N_Y, h, c))
        for y in range(N_Y)
        for h in range(N_HI)
        for c in range(N_CORE)
    ]


def in_hbm(x):
    return pltpu.with_memory_space_constraint(x, pltpu.HBM)


def chip_pairs(owners):
    return [
        [wide_at(y, h, c) * owners + n for c in range(N_CORE) for n in range(owners)]
        for y in range(N_Y)
        for h in range(N_HI)
    ]


HY_GROUPS = [[wide_at(y, h, c) for h in range(N_HI) for y in range(N_Y)] for c in range(N_CORE)]
N_X = 4


def offset_of(y, core):
    return 2 * (1 - core) if y < 4 else 1 + 2 * core, y % N_X


def shard_moves(owners):
    n_z = owners // N_X
    moves = []
    for y in range(N_Y):
        for h in range(N_HI):
            for c in range(N_CORE):
                dz, dx = offset_of(y, c)
                for z in range(n_z):
                    for x in range(N_X):
                        to = (z + dz) % n_z * N_X + (x + dx) % N_X
                        base = wide_at(y, h, c) * owners
                        moves.append((base + z * N_X + x, base + to))
    return moves


def call(body, out_shape, in_specs, scratch=(), flops=0, nbytes=0, limit=16):
    return pl.pallas_call(
        body,
        out_shape=out_shape,
        in_specs=in_specs,
        out_specs=jax.tree.map(lambda _: VMEM, out_shape),
        scratch_shapes=list(scratch),
        compiler_params=pltpu.CompilerParams(vmem_limit_bytes=limit * MIB),
        cost_estimate=pl.CostEstimate(flops=flops, bytes_accessed=nbytes, transcendentals=0),
    )


def join_body(first_ref, second_ref, out_ref, sems):
    inner = first_ref.shape[1]
    copies = [
        pltpu.make_async_copy(first_ref, out_ref.at[:, pl.ds(0, inner)], sems.at[0]),
        pltpu.make_async_copy(second_ref, out_ref.at[:, pl.ds(inner, second_ref.shape[1])], sems.at[1]),
    ]
    for copy in copies:
        copy.start()
    for copy in copies:
        copy.wait()


def tower_body(at_ref, *refs):
    whole, ahead, swapped = refs[0], refs[1:5], refs[5:9]
    pooled_hbm, cot_hbm, bias_ref, grad_ref, first, second, deltas, pooled_ref, cot_ref, sems = refs[9:]
    core, y, z, x = at_ref[0], at_ref[1], at_ref[2], at_ref[3]
    owners, rows, inner = first.shape
    top = second.shape[2]
    blocks = [(whole.at[0], 0, core), (whole.at[1], 0, 1 - core)]
    for k in range(1, 4):
        for part in range(N_CORE):
            blocks.append((ahead[k - 1].at[part], (2 * core - 1) * k, core if part == 0 else 1 - core))
            blocks.append((swapped[k - 1].at[part], (1 - 2 * core) * k, 1 - core if part == 0 else core))
    blocks.append((ahead[3], 4, core))
    blocks.append((swapped[3], 4, 1 - core))
    copies = [
        pltpu.make_async_copy(pooled_hbm, pooled_ref, sems.at[0, len(blocks)]),
        pltpu.make_async_copy(cot_hbm, cot_ref, sems.at[1, len(blocks)]),
    ]
    for p, (ref, shift, side) in enumerate(blocks):
        source = jnp.bitwise_and(y + shift + N_Y, N_Y - 1)
        dz = jnp.where(source < 4, 2 * (1 - side), 1 + 2 * side)
        from_z = jnp.bitwise_and(z - dz + 4, owners // N_X - 1)
        from_x = jnp.bitwise_and(x - source + N_Y, N_X - 1)
        owner = from_z * N_X + from_x
        copies.append(pltpu.make_async_copy(ref.at[:, pl.ds(0, inner)], first.at[owner], sems.at[0, p]))
        copies.append(pltpu.make_async_copy(ref.at[:, pl.ds(inner, top)], second.at[owner], sems.at[1, p]))
    for copy in copies:
        copy.start()
    for copy in copies:
        copy.wait()
    step = 256
    across = (((1,), (1,)), ((), ()))
    per = step // rows
    for k in range(inner // step):
        cols = slice(k * step, (k + 1) * step)
        columns = first[:, :, cols].reshape(owners * rows, step)
        units = second[k * per : (k + 1) * per].reshape(step, second.shape[2])
        hidden = jnp.dot(pooled_ref[...], columns, preferred_element_type=f32) + bias_ref[:, cols]
        back = lax.dot_general(cot_ref[...], units, across, preferred_element_type=f32)
        gate = jax.nn.sigmoid(hidden)
        deltas[:, cols] = (back * (gate * (1.0 + hidden * (1.0 - gate)))).astype(bf16)
    for k in range(owners * rows // step):
        features = first[k * per : (k + 1) * per].reshape(step, inner)
        grad_ref[:, k * step : (k + 1) * step] = lax.dot_general(
            deltas[...], features, across, preferred_element_type=f32
        ).astype(bf16)


def partial_body(counts_ref, grad_ref, out_ref):
    owners, tables, act, bags = counts_ref.shape
    emb = grad_ref.shape[1] // tables
    per = tables // out_ref.shape[0]
    for t in range(tables):
        lookups = counts_ref[:, t, :, :].reshape(owners * act, bags)
        part = jnp.dot(lookups, grad_ref[:, t * emb : (t + 1) * emb], preferred_element_type=f32)
        at = (t % per) * emb
        out_ref[t // per, :, :, at : at + emb] = part.reshape(owners, act, emb).astype(bf16)


def clip_body(scale, limit, parts_ref, out_ref, rows):
    groups, owners, act, width = parts_ref.shape
    emb = rows.shape[1]
    for g in range(groups):
        total = parts_ref[g, 0].astype(f32)
        for n in range(1, owners):
            total = total + parts_ref[g, n].astype(f32)
        total = total * scale
        for t in range(width // emb):
            grads = total[:, t * emb : (t + 1) * emb]
            norms = jnp.sqrt(jnp.sum(grads * grads, axis=-1, keepdims=True))
            clipped = grads * (limit / jnp.maximum(norms, limit))
            at = slice(t * act, (t + 1) * act)
            rows[at, :] = clipped if g == 0 else rows[at, :] + clipped
    both = rows[...].astype(bf16)
    for n in range(out_ref.shape[0]):
        out_ref[n] = both


def share_body(parts_ref, out_ref):
    total = parts_ref[0].astype(f32)
    for n in range(1, parts_ref.shape[0]):
        total = total + parts_ref[n].astype(f32)
    out_ref[...] = total


def update_body(at_ref, ids_ref, mine_ref, other_ref, table_ref, accum_ref, new_table_ref, new_accum_ref, dense):
    tables, act = ids_ref.shape
    per_core = tables // N_CORE
    core = at_ref[0]
    dense[...] = jnp.zeros_like(dense)
    for ref, side in ((mine_ref, core), (other_ref, 1 - core)):
        for t in range(per_core):
            for a in range(act):
                table = side * per_core + t
                row = ids_ref[table, a]
                dense[table, pl.ds(row, 1), :] = ref[pl.ds(t * act + a, 1), :]
    for t in range(tables):
        summed = dense[t]
        new_acc = accum_ref[t] + summed * summed
        new_accum_ref[t] = new_acc
        new_table_ref[t] = table_ref[t] - learn_rate * summed / (jnp.sqrt(new_acc) + epsilon)


def shards(pooled, cotangent, w_first, b_first, w_second, counts, row_ids, table, accum):
    tables, act, bags = counts.shape
    emb = table.shape[2]
    samples = pooled.shape[0]
    inner, top = w_first.shape[1], w_second.shape[1]
    owners = lax.axis_size("narrow")
    scale = 1.0 / math.sqrt(bags)
    limit = clip_factor * math.sqrt(emb)
    wide = lax.axis_index("wide").astype(jnp.int32)
    core = jnp.bitwise_and(wide, N_CORE - 1)
    y = jnp.right_shift(wide, 2)
    narrow = lax.axis_index("narrow").astype(jnp.int32)
    place = jnp.stack([core, y, jnp.right_shift(narrow, 2), jnp.bitwise_and(narrow, N_X - 1)])

    shard = call(
        join_body,
        jax.ShapeDtypeStruct((w_first.shape[0], inner + top), bf16),
        [HBM, HBM],
        [pltpu.SemaphoreType.DMA((2,))],
        nbytes=MIB // 2,
        limit=2,
    )(in_hbm(w_first), in_hbm(w_second))
    moved = lax.ppermute(shard, ("wide", "narrow"), shard_moves(owners))
    counts, _ = lax.optimization_barrier((counts, shard))
    by_owner = jnp.transpose(counts.reshape(tables, act, owners, samples), (2, 0, 1, 3))
    regrouped = lax.all_to_all(by_owner, "narrow", 0, 0, tiled=True)
    whole = jnp.stack([moved, lax.ppermute(moved, "wide", CORE_SWAP)])
    ahead2 = lax.ppermute(whole, "wide", y_shift(2))
    ahead1 = lax.ppermute(whole, "wide", y_shift(1))
    ahead3 = lax.ppermute(ahead2, "wide", y_shift(1))
    ahead4 = lax.ppermute(ahead2[0], "wide", y_shift(2))
    ring = [ahead1, ahead2, ahead3, ahead4]
    swapped = [lax.ppermute(block, "wide", CORE_SWAP) for block in ring]

    grad_in = call(
        tower_body,
        jax.ShapeDtypeStruct((samples, owners * w_first.shape[0]), bf16),
        [SMEM] + [HBM] * 11 + [VMEM],
        [
            pltpu.VMEM((owners, w_first.shape[0], inner), bf16),
            pltpu.VMEM((owners, w_second.shape[0], top), bf16),
            pltpu.VMEM((samples, inner), bf16),
            pltpu.VMEM(pooled.shape, bf16),
            pltpu.VMEM(cotangent.shape, bf16),
            pltpu.SemaphoreType.DMA((2, N_Y * N_CORE + 1)),
        ],
        flops=35 * samples * inner * (2 * inner + top) // 2,
        nbytes=8 * MIB,
    )(place, *map(in_hbm, (whole, *ring, *swapped, pooled, cotangent)), b_first.reshape(1, -1))

    quarters = N_CORE
    parts = call(
        partial_body,
        jax.ShapeDtypeStruct((quarters, owners, act, tables // quarters * emb), bf16),
        [VMEM] * 2,
        flops=2 * owners * act * samples * tables * emb,
        nbytes=4 * MIB,
    )(regrouped, grad_in)
    arrived = lax.all_to_all(
        parts.reshape(owners * quarters, act, -1),
        ("wide", "narrow"),
        0,
        0,
        axis_index_groups=chip_pairs(owners),
        tiled=True,
    )
    rows = tables * act // quarters
    copies = call(
        functools.partial(clip_body, scale, limit),
        jax.ShapeDtypeStruct((N_Y * N_HI, rows, emb), bf16),
        [VMEM],
        [pltpu.VMEM((rows, emb), f32)],
        nbytes=MIB,
    )(arrived.reshape(parts.shape))
    shares = lax.all_to_all(copies, "wide", 0, 0, axis_index_groups=HY_GROUPS, tiled=True)
    mine = call(share_body, jax.ShapeDtypeStruct((rows, emb), f32), [VMEM], nbytes=MIB)(shares)
    theirs = lax.ppermute(mine, "wide", CORE_SWAP)
    updated = jax.ShapeDtypeStruct(table.shape, f32)
    return call(
        update_body,
        (updated, updated),
        [SMEM, SMEM] + [VMEM] * 4,
        [pltpu.VMEM(table.shape, f32)],
        nbytes=2 * MIB,
    )(place, row_ids, mine, theirs, table, accum)


def solution(mesh):
    in_specs = (
        P(("wide", "narrow"), None),
        P(("wide", "narrow"), None),
        P("narrow", None),
        P(),
        P("narrow", None),
        P(None, "narrow", "wide"),
        P(None, "narrow"),
        P(None, "narrow", None),
        P(None, "narrow", None),
    )
    out_specs = (P(None, "narrow", None), P(None, "narrow", None))
    return jax.shard_map(shards, mesh=mesh, in_specs=in_specs, out_specs=out_specs, check_vma=False)
```

```python
import functools
import math

import jax
import jax.numpy as jnp
from jax import lax
from jax.experimental import pallas as pl
from jax.experimental.pallas import tpu as pltpu
from jax.sharding import PartitionSpec as P

clip_factor = 0.5
learn_rate = 0.05
epsilon = 1e-08

N_Y, N_HI, N_CORE = 8, 2, 2
bf16, f32 = jnp.bfloat16, jnp.float32
VMEM = pl.BlockSpec(memory_space=pltpu.VMEM)
SMEM = pl.BlockSpec(memory_space=pltpu.SMEM)
HBM = pl.BlockSpec(memory_space=pltpu.HBM)
MIB = 1 << 20


def wide_at(y, hi, core):
    return (y * N_HI + hi) * N_CORE + core


CORE_SWAP = [(w, w ^ 1) for w in range(N_Y * N_HI * N_CORE)]


def y_shift(by):
    return [
        (wide_at(y, h, c), wide_at((y + by - 2 * by * c) % N_Y, h, c))
        for y in range(N_Y)
        for h in range(N_HI)
        for c in range(N_CORE)
    ]


def in_hbm(x):
    return pltpu.with_memory_space_constraint(x, pltpu.HBM)


def chip_pairs(owners):
    return [
        [wide_at(y, h, c) * owners + n for c in range(N_CORE) for n in range(owners)]
        for y in range(N_Y)
        for h in range(N_HI)
    ]


HY_GROUPS = [[wide_at(y, h, c) for h in range(N_HI) for y in range(N_Y)] for c in range(N_CORE)]
N_X = 4


def offset_of(y, core):
    return 2 * (1 - core) if y < 4 else 1 + 2 * core, y % N_X


def shard_moves(owners):
    n_z = owners // N_X
    moves = []
    for y in range(N_Y):
        for h in range(N_HI):
            for c in range(N_CORE):
                dz, dx = offset_of(y, c)
                for z in range(n_z):
                    for x in range(N_X):
                        to = (z + dz) % n_z * N_X + (x + dx) % N_X
                        base = wide_at(y, h, c) * owners
                        moves.append((base + z * N_X + x, base + to))
    return moves


def call(body, out_shape, in_specs, scratch=(), flops=0, nbytes=0, limit=16, out=VMEM):
    return pl.pallas_call(
        body,
        out_shape=out_shape,
        in_specs=in_specs,
        out_specs=jax.tree.map(lambda _: out, out_shape),
        scratch_shapes=list(scratch),
        compiler_params=pltpu.CompilerParams(vmem_limit_bytes=limit * MIB),
        cost_estimate=pl.CostEstimate(flops=flops, bytes_accessed=nbytes, transcendentals=0),
    )


def join_body(first_ref, second_ref, out_ref, sems):
    inner = first_ref.shape[1]
    copies = [
        pltpu.make_async_copy(first_ref, out_ref.at[:, pl.ds(0, inner)], sems.at[0]),
        pltpu.make_async_copy(second_ref, out_ref.at[:, pl.ds(inner, second_ref.shape[1])], sems.at[1]),
    ]
    for copy in copies:
        copy.start()
    for copy in copies:
        copy.wait()


def regroup_body(counts_ref, out_ref, held, sems):
    owners, bags = held.shape[0], held.shape[3]
    reads = [
        pltpu.make_async_copy(counts_ref.at[:, :, pl.ds(n * bags, bags)], held.at[n], sems.at[0, n])
        for n in range(owners)
    ]
    writes = [pltpu.make_async_copy(held.at[n], out_ref.at[n], sems.at[1, n]) for n in range(owners)]
    for copy in reads:
        copy.start()
    for read, write in zip(reads, writes):
        read.wait()
        write.start()
    for copy in writes:
        copy.wait()


def tower_body(at_ref, *refs):
    whole, ahead, swapped = refs[0], refs[1:5], refs[5:9]
    pooled_hbm, cot_hbm, bias_ref, grad_ref, first, second, deltas, pooled_ref, cot_ref, sems = refs[9:]
    core, y, z, x = at_ref[0], at_ref[1], at_ref[2], at_ref[3]
    owners, rows, inner = first.shape
    top = second.shape[2]
    blocks = [(whole.at[0], 0, core), (whole.at[1], 0, 1 - core)]
    for k in range(1, 4):
        for part in range(N_CORE):
            blocks.append((ahead[k - 1].at[part], (2 * core - 1) * k, core if part == 0 else 1 - core))
            blocks.append((swapped[k - 1].at[part], (1 - 2 * core) * k, 1 - core if part == 0 else core))
    blocks.append((ahead[3], 4, core))
    blocks.append((swapped[3], 4, 1 - core))
    copies = [
        pltpu.make_async_copy(pooled_hbm, pooled_ref, sems.at[0, len(blocks)]),
        pltpu.make_async_copy(cot_hbm, cot_ref, sems.at[1, len(blocks)]),
    ]
    for p, (ref, shift, side) in enumerate(blocks):
        source = jnp.bitwise_and(y + shift + N_Y, N_Y - 1)
        dz = jnp.where(source < 4, 2 * (1 - side), 1 + 2 * side)
        from_z = jnp.bitwise_and(z - dz + 4, owners // N_X - 1)
        from_x = jnp.bitwise_and(x - source + N_Y, N_X - 1)
        owner = from_z * N_X + from_x
        copies.append(pltpu.make_async_copy(ref.at[:, pl.ds(0, inner)], first.at[owner], sems.at[0, p]))
        copies.append(pltpu.make_async_copy(ref.at[:, pl.ds(inner, top)], second.at[owner], sems.at[1, p]))
    for copy in copies:
        copy.start()
    for copy in copies:
        copy.wait()
    step = 256
    across = (((1,), (1,)), ((), ()))
    per = step // rows
    for k in range(inner // step):
        cols = slice(k * step, (k + 1) * step)
        columns = first[:, :, cols].reshape(owners * rows, step)
        units = second[k * per : (k + 1) * per].reshape(step, second.shape[2])
        hidden = jnp.dot(pooled_ref[...], columns, preferred_element_type=f32) + bias_ref[:, cols]
        back = lax.dot_general(cot_ref[...], units, across, preferred_element_type=f32)
        gate = jax.nn.sigmoid(hidden)
        deltas[:, cols] = (back * (gate * (1.0 + hidden * (1.0 - gate)))).astype(bf16)
    for k in range(owners * rows // step):
        features = first[k * per : (k + 1) * per].reshape(step, inner)
        grad_ref[:, k * step : (k + 1) * step] = lax.dot_general(
            deltas[...], features, across, preferred_element_type=f32
        ).astype(bf16)


def partial_body(counts_ref, grad_ref, out_ref):
    owners, tables, act, bags = counts_ref.shape
    emb = grad_ref.shape[1] // tables
    per = tables // out_ref.shape[0]
    for t in range(tables):
        lookups = counts_ref[:, t, :, :].reshape(owners * act, bags)
        part = jnp.dot(lookups, grad_ref[:, t * emb : (t + 1) * emb], preferred_element_type=f32)
        at = (t % per) * emb
        out_ref[t // per, :, :, at : at + emb] = part.reshape(owners, act, emb).astype(bf16)


def clip_body(scale, limit, parts_ref, out_ref, rows):
    groups, owners, act, width = parts_ref.shape
    emb = rows.shape[1]
    for g in range(groups):
        total = parts_ref[g, 0].astype(f32)
        for n in range(1, owners):
            total = total + parts_ref[g, n].astype(f32)
        total = total * scale
        for t in range(width // emb):
            grads = total[:, t * emb : (t + 1) * emb]
            norms = jnp.sqrt(jnp.sum(grads * grads, axis=-1, keepdims=True))
            clipped = grads * (limit / jnp.maximum(norms, limit))
            at = slice(t * act, (t + 1) * act)
            rows[at, :] = clipped if g == 0 else rows[at, :] + clipped
    both = rows[...].astype(bf16)
    for n in range(out_ref.shape[0]):
        out_ref[n] = both


def share_body(parts_ref, out_ref):
    total = parts_ref[0].astype(f32)
    for n in range(1, parts_ref.shape[0]):
        total = total + parts_ref[n].astype(f32)
    out_ref[...] = total


def update_body(at_ref, ids_ref, mine_ref, other_ref, table_ref, accum_ref, new_table_ref, new_accum_ref, dense):
    tables, act = ids_ref.shape
    per_core = tables // N_CORE
    core = at_ref[0]
    dense[...] = jnp.zeros_like(dense)
    for ref, side in ((mine_ref, core), (other_ref, 1 - core)):
        for t in range(per_core):
            for a in range(act):
                table = side * per_core + t
                row = ids_ref[table, a]
                dense[table, pl.ds(row, 1), :] = ref[pl.ds(t * act + a, 1), :]
    for t in range(tables):
        summed = dense[t]
        new_acc = accum_ref[t] + summed * summed
        new_accum_ref[t] = new_acc
        new_table_ref[t] = table_ref[t] - learn_rate * summed / (jnp.sqrt(new_acc) + epsilon)


def shards(pooled, cotangent, w_first, b_first, w_second, counts, row_ids, table, accum):
    tables, act, bags = counts.shape
    emb = table.shape[2]
    samples = pooled.shape[0]
    inner, top = w_first.shape[1], w_second.shape[1]
    owners = lax.axis_size("narrow")
    scale = 1.0 / math.sqrt(bags)
    limit = clip_factor * math.sqrt(emb)
    wide = lax.axis_index("wide").astype(jnp.int32)
    core = jnp.bitwise_and(wide, N_CORE - 1)
    y = jnp.right_shift(wide, 2)
    narrow = lax.axis_index("narrow").astype(jnp.int32)
    place = jnp.stack([core, y, jnp.right_shift(narrow, 2), jnp.bitwise_and(narrow, N_X - 1)])

    shard = call(
        join_body,
        jax.ShapeDtypeStruct((w_first.shape[0], inner + top), bf16),
        [HBM, HBM],
        [pltpu.SemaphoreType.DMA((2,))],
        nbytes=MIB // 2,
        limit=2,
    )(in_hbm(w_first), in_hbm(w_second))
    moved = lax.ppermute(shard, ("wide", "narrow"), shard_moves(owners))
    counts, _ = lax.optimization_barrier((counts, shard))
    by_owner = call(
        regroup_body,
        pltpu.HBM((owners, tables, act, samples), bf16),
        [HBM],
        [pltpu.VMEM((owners, tables, act, samples), bf16), pltpu.SemaphoreType.DMA((2, owners))],
        nbytes=4 * MIB,
        limit=8,
        out=HBM,
    )(in_hbm(counts))
    regrouped = lax.all_to_all(by_owner, "narrow", 0, 0, tiled=True)
    whole = jnp.stack([moved, lax.ppermute(moved, "wide", CORE_SWAP)])
    ahead2 = lax.ppermute(whole, "wide", y_shift(2))
    ahead1 = lax.ppermute(whole, "wide", y_shift(1))
    ahead3 = lax.ppermute(ahead2, "wide", y_shift(1))
    ahead4 = lax.ppermute(ahead2[0], "wide", y_shift(2))
    ring = [ahead1, ahead2, ahead3, ahead4]
    swapped = [lax.ppermute(block, "wide", CORE_SWAP) for block in ring]

    grad_in = call(
        tower_body,
        jax.ShapeDtypeStruct((samples, owners * w_first.shape[0]), bf16),
        [SMEM] + [HBM] * 11 + [VMEM],
        [
            pltpu.VMEM((owners, w_first.shape[0], inner), bf16),
            pltpu.VMEM((owners, w_second.shape[0], top), bf16),
            pltpu.VMEM((samples, inner), bf16),
            pltpu.VMEM(pooled.shape, bf16),
            pltpu.VMEM(cotangent.shape, bf16),
            pltpu.SemaphoreType.DMA((2, N_Y * N_CORE + 1)),
        ],
        flops=34 * samples * inner * (2 * inner + top) // 2,
        nbytes=8 * MIB,
    )(place, *map(in_hbm, (whole, *ring, *swapped, pooled, cotangent)), b_first.reshape(1, -1))

    quarters = N_CORE
    parts = call(
        partial_body,
        jax.ShapeDtypeStruct((quarters, owners, act, tables // quarters * emb), bf16),
        [VMEM] * 2,
        flops=2 * owners * act * samples * tables * emb,
        nbytes=4 * MIB,
    )(regrouped, grad_in)
    arrived = lax.all_to_all(
        parts.reshape(owners * quarters, act, -1),
        ("wide", "narrow"),
        0,
        0,
        axis_index_groups=chip_pairs(owners),
        tiled=True,
    )
    rows = tables * act // quarters
    copies = call(
        functools.partial(clip_body, scale, limit),
        jax.ShapeDtypeStruct((N_Y * N_HI, rows, emb), bf16),
        [VMEM],
        [pltpu.VMEM((rows, emb), f32)],
        nbytes=MIB,
    )(arrived.reshape(parts.shape))
    shares = lax.all_to_all(copies, "wide", 0, 0, axis_index_groups=HY_GROUPS, tiled=True)
    mine = call(share_body, jax.ShapeDtypeStruct((rows, emb), f32), [VMEM], nbytes=MIB)(shares)
    theirs = lax.ppermute(mine, "wide", CORE_SWAP)
    updated = jax.ShapeDtypeStruct(table.shape, f32)
    return call(
        update_body,
        (updated, updated),
        [SMEM, SMEM] + [VMEM] * 4,
        [pltpu.VMEM(table.shape, f32)],
        nbytes=2 * MIB,
    )(place, row_ids, mine, theirs, table, accum)


def solution(mesh):
    in_specs = (
        P(("wide", "narrow"), None),
        P(("wide", "narrow"), None),
        P("narrow", None),
        P(),
        P("narrow", None),
        P(None, "narrow", "wide"),
        P(None, "narrow"),
        P(None, "narrow", None),
        P(None, "narrow", None),
    )
    out_specs = (P(None, "narrow", None), P(None, "narrow", None))
    return jax.shard_map(shards, mesh=mesh, in_specs=in_specs, out_specs=out_specs, check_vma=False)
```

```python
import functools
import math

import jax
import jax.numpy as jnp
from jax import lax
from jax.experimental import pallas as pl
from jax.experimental.pallas import tpu as pltpu
from jax.sharding import PartitionSpec as P

clip_factor = 0.5
learn_rate = 0.05
epsilon = 1e-08

N_Y, N_HI, N_CORE = 8, 2, 2
bf16, f32 = jnp.bfloat16, jnp.float32
VMEM = pl.BlockSpec(memory_space=pltpu.VMEM)
SMEM = pl.BlockSpec(memory_space=pltpu.SMEM)
HBM = pl.BlockSpec(memory_space=pltpu.HBM)
MIB = 1 << 20


def wide_at(y, hi, core):
    return (y * N_HI + hi) * N_CORE + core


CORE_SWAP = [(w, w ^ 1) for w in range(N_Y * N_HI * N_CORE)]


def y_shift(by):
    return [
        (wide_at(y, h, c), wide_at((y + by - 2 * by * c) % N_Y, h, c))
        for y in range(N_Y)
        for h in range(N_HI)
        for c in range(N_CORE)
    ]


def in_hbm(x):
    return pltpu.with_memory_space_constraint(x, pltpu.HBM)


def chip_pairs(owners):
    return [
        [wide_at(y, h, c) * owners + n for c in range(N_CORE) for n in range(owners)]
        for y in range(N_Y)
        for h in range(N_HI)
    ]


HY_GROUPS = [[wide_at(y, h, c) for h in (1, 0) for y in range(N_Y - 1, -1, -1)] for c in range(N_CORE)]
N_X = 4


def offset_of(y, core):
    return 2 * (1 - core) if y < 4 else 1 + 2 * core, y % N_X


def shard_moves(owners):
    n_z = owners // N_X
    moves = []
    for y in range(N_Y):
        for h in range(N_HI):
            for c in range(N_CORE):
                dz, dx = offset_of(y, c)
                for z in range(n_z):
                    for x in range(N_X):
                        to = (z + dz) % n_z * N_X + (x + dx) % N_X
                        base = wide_at(y, h, c) * owners
                        moves.append((base + z * N_X + x, base + to))
    return moves


def call(body, out_shape, in_specs, scratch=(), flops=0, nbytes=0, limit=16, out=VMEM):
    return pl.pallas_call(
        body,
        out_shape=out_shape,
        in_specs=in_specs,
        out_specs=jax.tree.map(lambda _: out, out_shape),
        scratch_shapes=list(scratch),
        compiler_params=pltpu.CompilerParams(vmem_limit_bytes=limit * MIB),
        cost_estimate=pl.CostEstimate(flops=flops, bytes_accessed=nbytes, transcendentals=0),
    )


def join_body(first_ref, second_ref, out_ref, sems):
    inner = first_ref.shape[1]
    copies = [
        pltpu.make_async_copy(first_ref, out_ref.at[:, pl.ds(0, inner)], sems.at[0]),
        pltpu.make_async_copy(second_ref, out_ref.at[:, pl.ds(inner, second_ref.shape[1])], sems.at[1]),
    ]
    for copy in copies:
        copy.start()
    for copy in copies:
        copy.wait()


def regroup_body(counts_ref, out_ref, held, sems):
    owners, bags = held.shape[0], held.shape[3]
    reads = [
        pltpu.make_async_copy(counts_ref.at[:, :, pl.ds(n * bags, bags)], held.at[n], sems.at[0, n])
        for n in range(owners)
    ]
    writes = [pltpu.make_async_copy(held.at[n], out_ref.at[n], sems.at[1, n]) for n in range(owners)]
    for copy in reads:
        copy.start()
    for read, write in zip(reads, writes):
        read.wait()
        write.start()
    for copy in writes:
        copy.wait()


def tower_body(at_ref, *refs):
    whole, ahead, swapped = refs[0], refs[1:5], refs[5:9]
    pooled_hbm, cot_hbm, bias_ref, grad_ref, first, second, deltas, pooled_ref, cot_ref, sems = refs[9:]
    core, y, z, x = at_ref[0], at_ref[1], at_ref[2], at_ref[3]
    owners, rows, inner = first.shape
    top = second.shape[2]
    blocks = [(whole.at[0], 0, core), (whole.at[1], 0, 1 - core)]
    for k in range(1, 4):
        for part in range(N_CORE):
            blocks.append((ahead[k - 1].at[part], (2 * core - 1) * k, core if part == 0 else 1 - core))
            blocks.append((swapped[k - 1].at[part], (1 - 2 * core) * k, 1 - core if part == 0 else core))
    blocks.append((ahead[3], 4, core))
    blocks.append((swapped[3], 4, 1 - core))
    copies = [
        pltpu.make_async_copy(pooled_hbm, pooled_ref, sems.at[0, len(blocks)]),
        pltpu.make_async_copy(cot_hbm, cot_ref, sems.at[1, len(blocks)]),
    ]
    for p, (ref, shift, side) in enumerate(blocks):
        source = jnp.bitwise_and(y + shift + N_Y, N_Y - 1)
        dz = jnp.where(source < 4, 2 * (1 - side), 1 + 2 * side)
        from_z = jnp.bitwise_and(z - dz + 4, owners // N_X - 1)
        from_x = jnp.bitwise_and(x - source + N_Y, N_X - 1)
        owner = from_z * N_X + from_x
        copies.append(pltpu.make_async_copy(ref.at[:, pl.ds(0, inner)], first.at[owner], sems.at[0, p]))
        copies.append(pltpu.make_async_copy(ref.at[:, pl.ds(inner, top)], second.at[owner], sems.at[1, p]))
    for copy in copies:
        copy.start()
    for copy in copies:
        copy.wait()
    step = 256
    across = (((1,), (1,)), ((), ()))
    per = step // rows
    for k in range(inner // step):
        cols = slice(k * step, (k + 1) * step)
        columns = first[:, :, cols].reshape(owners * rows, step)
        units = second[k * per : (k + 1) * per].reshape(step, second.shape[2])
        hidden = jnp.dot(pooled_ref[...], columns, preferred_element_type=f32) + bias_ref[:, cols]
        back = lax.dot_general(cot_ref[...], units, across, preferred_element_type=f32)
        gate = jax.nn.sigmoid(hidden)
        deltas[:, cols] = (back * (gate * (1.0 + hidden * (1.0 - gate)))).astype(bf16)
    for k in range(owners * rows // step):
        features = first[k * per : (k + 1) * per].reshape(step, inner)
        grad_ref[:, k * step : (k + 1) * step] = lax.dot_general(
            deltas[...], features, across, preferred_element_type=f32
        ).astype(bf16)


def partial_body(counts_ref, grad_ref, out_ref):
    owners, tables, act, bags = counts_ref.shape
    emb = grad_ref.shape[1] // tables
    per = tables // out_ref.shape[0]
    for t in range(tables):
        lookups = counts_ref[:, t, :, :].reshape(owners * act, bags)
        part = jnp.dot(lookups, grad_ref[:, t * emb : (t + 1) * emb], preferred_element_type=f32)
        at = (t % per) * emb
        out_ref[t // per, :, :, at : at + emb] = part.reshape(owners, act, emb).astype(bf16)


def clip_body(scale, limit, parts_ref, out_ref, rows):
    groups, owners, act, width = parts_ref.shape
    emb = rows.shape[1]
    for g in range(groups):
        total = parts_ref[g, 0].astype(f32)
        for n in range(1, owners):
            total = total + parts_ref[g, n].astype(f32)
        total = total * scale
        for t in range(width // emb):
            grads = total[:, t * emb : (t + 1) * emb]
            norms = jnp.sqrt(jnp.sum(grads * grads, axis=-1, keepdims=True))
            clipped = grads * (limit / jnp.maximum(norms, limit))
            at = slice(t * act, (t + 1) * act)
            rows[at, :] = clipped if g == 0 else rows[at, :] + clipped
    both = rows[...].astype(bf16)
    for n in range(out_ref.shape[0]):
        out_ref[n] = both


def share_body(parts_ref, out_ref):
    total = parts_ref[0].astype(f32)
    for n in range(1, parts_ref.shape[0]):
        total = total + parts_ref[n].astype(f32)
    out_ref[...] = total


def update_body(at_ref, ids_ref, mine_ref, other_ref, table_ref, accum_ref, new_table_ref, new_accum_ref, dense):
    tables, act = ids_ref.shape
    per_core = tables // N_CORE
    core = at_ref[0]
    dense[...] = jnp.zeros_like(dense)
    for ref, side in ((mine_ref, core), (other_ref, 1 - core)):
        for t in range(per_core):
            for a in range(act):
                table = side * per_core + t
                row = ids_ref[table, a]
                dense[table, pl.ds(row, 1), :] = ref[pl.ds(t * act + a, 1), :]
    for t in range(tables):
        summed = dense[t]
        new_acc = accum_ref[t] + summed * summed
        new_accum_ref[t] = new_acc
        new_table_ref[t] = table_ref[t] - learn_rate * summed / (jnp.sqrt(new_acc) + epsilon)


def shards(pooled, cotangent, w_first, b_first, w_second, counts, row_ids, table, accum):
    tables, act, bags = counts.shape
    emb = table.shape[2]
    samples = pooled.shape[0]
    inner, top = w_first.shape[1], w_second.shape[1]
    owners = lax.axis_size("narrow")
    scale = 1.0 / math.sqrt(bags)
    limit = clip_factor * math.sqrt(emb)
    wide = lax.axis_index("wide").astype(jnp.int32)
    core = jnp.bitwise_and(wide, N_CORE - 1)
    y = jnp.right_shift(wide, 2)
    narrow = lax.axis_index("narrow").astype(jnp.int32)
    place = jnp.stack([core, y, jnp.right_shift(narrow, 2), jnp.bitwise_and(narrow, N_X - 1)])

    shard = call(
        join_body,
        jax.ShapeDtypeStruct((w_first.shape[0], inner + top), bf16),
        [HBM, HBM],
        [pltpu.SemaphoreType.DMA((2,))],
        nbytes=MIB // 2,
        limit=2,
    )(in_hbm(w_first), in_hbm(w_second))
    moved = lax.ppermute(shard, ("wide", "narrow"), shard_moves(owners))
    counts, _ = lax.optimization_barrier((counts, shard))
    by_owner = call(
        regroup_body,
        pltpu.HBM((owners, tables, act, samples), bf16),
        [HBM],
        [pltpu.VMEM((owners, tables, act, samples), bf16), pltpu.SemaphoreType.DMA((2, owners))],
        nbytes=4 * MIB,
        limit=8,
        out=HBM,
    )(in_hbm(counts))
    regrouped = lax.all_to_all(by_owner, "narrow", 0, 0, tiled=True)
    whole = jnp.stack([moved, lax.ppermute(moved, "wide", CORE_SWAP)])
    ahead2 = lax.ppermute(whole, "wide", y_shift(2))
    ahead1 = lax.ppermute(whole, "wide", y_shift(1))
    ahead3 = lax.ppermute(ahead2, "wide", y_shift(1))
    ahead4 = lax.ppermute(ahead2[0], "wide", y_shift(2))
    ring = [ahead1, ahead2, ahead3, ahead4]
    swapped = [lax.ppermute(block, "wide", CORE_SWAP) for block in ring]

    grad_in = call(
        tower_body,
        jax.ShapeDtypeStruct((samples, owners * w_first.shape[0]), bf16),
        [SMEM] + [HBM] * 11 + [VMEM],
        [
            pltpu.VMEM((owners, w_first.shape[0], inner), bf16),
            pltpu.VMEM((owners, w_second.shape[0], top), bf16),
            pltpu.VMEM((samples, inner), bf16),
            pltpu.VMEM(pooled.shape, bf16),
            pltpu.VMEM(cotangent.shape, bf16),
            pltpu.SemaphoreType.DMA((2, N_Y * N_CORE + 1)),
        ],
        flops=34 * samples * inner * (2 * inner + top) // 2,
        nbytes=8 * MIB,
    )(place, *map(in_hbm, (whole, *ring, *swapped, pooled, cotangent)), b_first.reshape(1, -1))

    quarters = N_CORE
    parts = call(
        partial_body,
        jax.ShapeDtypeStruct((quarters, owners, act, tables // quarters * emb), bf16),
        [VMEM] * 2,
        flops=2 * owners * act * samples * tables * emb,
        nbytes=4 * MIB,
    )(regrouped, grad_in)
    arrived = lax.all_to_all(
        parts.reshape(owners * quarters, act, -1),
        ("wide", "narrow"),
        0,
        0,
        axis_index_groups=chip_pairs(owners),
        tiled=True,
    )
    rows = tables * act // quarters
    copies = call(
        functools.partial(clip_body, scale, limit),
        jax.ShapeDtypeStruct((N_Y * N_HI, rows, emb), bf16),
        [VMEM],
        [pltpu.VMEM((rows, emb), f32)],
        nbytes=MIB,
    )(arrived.reshape(parts.shape))
    shares = lax.all_to_all(copies, "wide", 0, 0, axis_index_groups=HY_GROUPS, tiled=True)
    mine = call(share_body, jax.ShapeDtypeStruct((rows, emb), f32), [VMEM], nbytes=MIB)(shares)
    theirs = lax.ppermute(mine, "wide", CORE_SWAP)
    updated = jax.ShapeDtypeStruct(table.shape, f32)
    return call(
        update_body,
        (updated, updated),
        [SMEM, SMEM] + [VMEM] * 4,
        [pltpu.VMEM(table.shape, f32)],
        nbytes=2 * MIB,
    )(place, row_ids, mine, theirs, table, accum)


def solution(mesh):
    in_specs = (
        P(("wide", "narrow"), None),
        P(("wide", "narrow"), None),
        P("narrow", None),
        P(),
        P("narrow", None),
        P(None, "narrow", "wide"),
        P(None, "narrow"),
        P(None, "narrow", None),
        P(None, "narrow", None),
    )
    out_specs = (P(None, "narrow", None), P(None, "narrow", None))
    return jax.shard_map(shards, mesh=mesh, in_specs=in_specs, out_specs=out_specs, check_vma=False)
```
